256 devices in a mesh: gx: 16 (over z, core), gy: 4 (over y), gz: 4 (over x).
Axes of the slice: x: 4, y: 4, z: 8, core: 2. Of those that a mesh axis runs over, the one named last changes fastest.
Arguments:
- velocity: float32 [3, 128, 128, 512], P(None, 'gx', 'gy', 'gz'), may hold values from -6 to 6
- nu_tilde: float32 [128, 128, 512], P('gx', 'gy', 'gz'), may hold values from 0.05 to 2
- fluid_cells: int32 [128, 128, 512], P('gx', 'gy', 'gz'), may hold values 0 or 1
- surface: float32 [16, 4, 3, 512], P('gx', 'gz', None, 'gy'), may hold values from -64 to 64
- pitch_angle: float32 [1], replicated, may hold values from -0.15 to 0.15
- near_tiles: int32 [16, 4, 4, 8], P('gx', 'gy', 'gz'), may hold values from -1 to 31, as said below
- send_rows: int32 [16, 4, 4, 64, 128], P('gx', 'gy', 'gz'), may hold values from -1 to 32767, as said below
- ghost_cell: int32 [16, 4, 4, 2048], P('gx', 'gy', 'gz'), may hold values from 0 to 32767, as said below
- ghost_src: int32 [16, 4, 4, 8, 2048], P('gx', 'gy', 'gz'), may hold values from 0 to 8191, as said below
- ghost_weight: float32 [16, 4, 4, 8, 2048], P('gx', 'gy', 'gz'), may hold values from 0 to 1, as said below
Outputs:
- new_velocity: float32 [3, 128, 128, 512], P(None, 'gx', 'gy', 'gz')
- new_nu_tilde: float32 [128, 128, 512], P('gx', 'gy', 'gz')
- wall_distance: float32 [128, 128, 512], P('gx', 'gy', 'gz')
The draws below stay inside these ranges and needn't reach their ends.
Inputs may be any that keep to these rules, and one draw needn't show every extreme that they name: `send_rows`: in each list of 128 slots from one device to one peer of gx+gz, live entries (local cell numbers of the sender) come first and the rest are -1. In every spanwise index some peer receives 128 live rows from every device. `ghost_src`: p * 128 + s names slot s of the rows that peer p sends to this device; it always names a live slot. `ghost_cell`: the 2048 entries of one device are distinct. `near_tiles`: distinct tiles first, the rest -1; some device lists 8 tiles. `ghost_weight`: the weights of one image point are non-negative and sum to one.
All inputs are finite; a program needn't handle non-finite values. No bound on the sum of `fluid_cells` on one device may be relied on, other than what follows from the above.
Results may differ from the reference program's by a relative error of at most 0.0003.
Values sent between devices are 32-bit elements; how exact they have to be, the bound alone decides.
No kernel may reach another device: no remote copies, remote signals or barrier semaphores. Data moves between devices by JAX's collectives and lax.ppermute only.
A program may use at most 128 MiB of HBM per device.

```python
import math
import jax
import jax.numpy as jnp
from jax import lax

CX = 8
CY = 32
CZ = 128
TY = 8
STENCIL = 8
TRI_DEV = 128
CAP = 128
GHOSTS = 2048
NEAR_MAX = 8
NX = 128
NY = 128
NZ = 512
PEERS = 64
N_GX = 16
N_GY = 4
N_GZ = 4


def route_counts(key):
    base_key = jax.random.fold_in(key, 977)
    key_one, key_two = jax.random.split(base_key)
    peer_total = N_GX * N_GZ
    base_count = jax.random.randint(key_one, (N_GX, N_GY, N_GZ, peer_total), CAP // 2, CAP + 1)
    busiest = jax.random.randint(key_two, (N_GY,), 0, peer_total)
    target = jnp.arange(peer_total, dtype=jnp.int32)
    is_full = target[None, None, None, :] == busiest[None, :, None, None]
    return jnp.where(is_full, CAP, base_count).astype(jnp.int32)


def draw_send_rows(key, part):
    counts = route_counts(key)
    key = jax.random.fold_in(key, 3)
    chosen = jax.random.randint(key, (N_GX, N_GY, N_GZ, N_GX * N_GZ, CAP), 0, CX * CY * CZ)
    slot_index = jnp.arange(CAP, dtype=jnp.int32)
    return jnp.where(slot_index < counts[..., None], chosen, -1).astype(jnp.int32)


def draw_ghost_src(key, part):
    counts = route_counts(key)
    key = jax.random.fold_in(key, 5)
    key_one, key_two = jax.random.split(key)
    peer_total = N_GX * N_GZ
    full_shape = (N_GX, N_GY, N_GZ, STENCIL, GHOSTS)
    source = jax.random.randint(key_one, full_shape, 0, peer_total)
    count_table = counts.transpose(1, 0, 2, 3).reshape(N_GY, peer_total, peer_total)
    receiver = jnp.arange(N_GX, dtype=jnp.int32)[:, None] * N_GZ + jnp.arange(N_GZ, dtype=jnp.int32)[None, :]
    span_index = jnp.arange(N_GY, dtype=jnp.int32)
    slot_limit = count_table[span_index[None, :, None, None, None], source, receiver[:, None, :, None, None]]
    offset = jax.random.randint(key_two, full_shape, 0, slot_limit)
    return (source * CAP + offset).astype(jnp.int32)


def draw_ghost_cell(key, part):
    key = jax.random.fold_in(key, 7)
    key_list = jax.random.split(key, N_GX * N_GY * N_GZ)
    chosen = jax.vmap(lambda subkey: jax.random.permutation(subkey, CX * CY * CZ)[:GHOSTS])(key_list)
    return chosen.reshape(N_GX, N_GY, N_GZ, GHOSTS).astype(jnp.int32)


def draw_near_tiles(key, part):
    key = jax.random.fold_in(key, 11)
    key_one, key_two, key_three = jax.random.split(key, 3)
    devices = N_GX * N_GY * N_GZ
    tile_count = CX * (CY // TY)
    key_list = jax.random.split(key_one, devices)
    chosen = jax.vmap(lambda subkey: jax.random.permutation(subkey, tile_count)[:NEAR_MAX])(key_list)
    counts = jax.random.randint(key_two, (devices,), 1, NEAR_MAX + 1)
    fullest = jax.random.randint(key_three, (), 0, devices)
    counts = jnp.where(jnp.arange(devices, dtype=jnp.int32) == fullest, NEAR_MAX, counts)
    slot_index = jnp.arange(NEAR_MAX, dtype=jnp.int32)
    listed = jnp.where(slot_index[None, :] < counts[:, None], chosen, -1)
    return listed.reshape(N_GX, N_GY, N_GZ, NEAR_MAX).astype(jnp.int32)


def draw_surface(key, part):
    key = jax.random.fold_in(key, 13)
    unit_draw = jax.random.uniform(key, (N_GX, N_GZ, 3, TRI_DEV * N_GY), jnp.float32, -1.0, 1.0)
    extent = jnp.array([0.5 * CX, 0.5 * CY * N_GY, 0.5 * CZ], jnp.float32)
    return unit_draw * extent[None, None, :, None]


def draw_ghost_weight(key, part):
    key = jax.random.fold_in(key, 17)
    fraction = jax.random.uniform(key, (N_GX, N_GY, N_GZ, 3, GHOSTS), jnp.float32)
    corners = []
    for corner in range(8):
        weight = jnp.ones_like(fraction[:, :, :, 0])
        for direction in range(3):
            if corner >> direction & 1:
                weight = weight * fraction[:, :, :, direction]
            else:
                weight = weight * (1.0 - fraction[:, :, :, direction])
        corners.append(weight)
    return jnp.stack(corners, axis=3)


def with_ends(result, key, smallest, high):
    place = [jax.random.randint(jax.random.fold_in(key, axis), (), 0, length) for axis, length in enumerate(result.shape)]
    widest = result.shape.index(max(result.shape))
    beside = place[:widest] + [(place[widest] + 1) % result.shape[widest]] + place[widest + 1:]
    return result.at[tuple(place)].set(smallest).at[tuple(beside)].set(high)


def shard_levels(rng, shape, shards, low, largest):
    gain, own = 1.0, jax.random.fold_in(rng, 6)
    for position, blocks in shards:
        heights = jnp.exp(jax.random.uniform(jax.random.fold_in(own, position), (blocks,), jnp.float32, low / len(shards), largest / len(shards)))
        gain = gain * jnp.repeat(heights, shape[position] // blocks).reshape([-1 if axis == position else 1 for axis in range(len(shape))])
    return gain


def gaussian(rng, shape, deviation, bound, cuts=(), kind=jnp.bfloat16):
    result = jax.random.normal(rng, shape, jnp.float32) * deviation
    if len(cuts) > 0:
        result = shard_levels(rng, shape, cuts, -0.22, 0.18) * result
    return jnp.clip(result, min=-bound, max=bound).astype(kind)


def setup_inputs(seed: int = 0) -> dict:
    streams_of = jax.random.split(jax.random.key(seed), 11)
    velocity = gaussian(streams_of[0], (3, NX, NY, NZ), 1.0, 6.0, ((1, 16), (2, 4), (3, 4)), jnp.float32)
    nu_tilde = jnp.clip(jnp.exp(math.log(2.0) - 3.6888794 * jax.random.uniform(streams_of[1], (NX, NY, NZ), jnp.float32) ** shard_levels(streams_of[1], (NX, NY, NZ), ((0, 16), (1, 4), (2, 4)), -0.2, 0.2)), 0.05, 2.0)
    fluid_cells = with_ends((jax.random.randint(streams_of[2], (NX, NY, NZ), 0, 8) < 7).astype(jnp.int32), jax.random.fold_in(streams_of[2], 1), 0, 1)
    surface = draw_surface(jax.random.fold_in(streams_of[10], 71), 0)
    pitch_angle = jnp.clip(jax.random.uniform(streams_of[4], (1,), jnp.float32, -0.15, 0.15), -0.15, 0.15)
    near_tiles = draw_near_tiles(jax.random.fold_in(streams_of[10], 71), 0)
    send_rows = draw_send_rows(jax.random.fold_in(streams_of[10], 71), 0)
    ghost_cell = draw_ghost_cell(jax.random.fold_in(streams_of[10], 71), 0)
    ghost_src = draw_ghost_src(jax.random.fold_in(streams_of[10], 71), 0)
    ghost_weight = draw_ghost_weight(jax.random.fold_in(streams_of[10], 71), 0)
    return {"velocity": velocity, "nu_tilde": nu_tilde, "fluid_cells": fluid_cells, "surface": surface, "pitch_angle": pitch_angle, "near_tiles": near_tiles, "send_rows": send_rows, "ghost_cell": ghost_cell, "ghost_src": ghost_src, "ghost_weight": ghost_weight}


viscosity = 0.2
prod_coef = 0.1355
grad_coef = 0.622
sigma_inv = 1.5
karman = 0.41
visc_coef = 7.1
wall_coef = prod_coef / (karman * karman) + (1.0 + grad_coef) * sigma_inv
des_coef = 0.65
floor_rate = 0.3
dist_eps = 0.25
dist_cap = 8.0
time_step = 0.05

def to_blocks(fields):
    components = fields.shape[0]
    shaped = fields.reshape(components, N_GX, CX, N_GY, CY, N_GZ, CZ)
    shaped = shaped.transpose(1, 3, 5, 0, 2, 4, 6)
    return shaped.reshape(N_GX, N_GY, N_GZ, components, CX * CY * CZ)

def from_blocks(blocks):
    components = blocks.shape[3]
    shaped = blocks.reshape(N_GX, N_GY, N_GZ, components, CX, CY, CZ)
    shaped = shaped.transpose(3, 0, 4, 1, 5, 2, 6)
    return shaped.reshape(components, N_GX * CX, N_GY * CY, N_GZ * CZ)

def rotate(points, pitch_angle):
    cosine = jnp.cos(pitch_angle[0])
    sine_value = jnp.sin(pitch_angle[0])
    turned_x = cosine * points[0] + sine_value * points[2]
    turned_z = cosine * points[2] - sine_value * points[0]
    return jnp.stack([turned_x, points[1], turned_z])

def cell_coords(tile_list, y_offset, total_span, cells_x, cells_y, cells_z):
    per_row = cells_y // TY
    slots = tile_list.shape[0]
    safe_tiles = jnp.maximum(tile_list, 0)
    plane_index = (safe_tiles // per_row).astype(jnp.float32)
    band_row = safe_tiles % per_row * TY + y_offset
    row_index = band_row[:, None] + jnp.arange(TY, dtype=jnp.int32)[None, :]
    coord_x = jnp.broadcast_to((plane_index + 0.5 - 0.5 * cells_x)[:, None, None], (slots, TY, cells_z))
    coord_y = jnp.broadcast_to((row_index.astype(jnp.float32) + 0.5 - 0.5 * total_span)[:, :, None], (slots, TY, cells_z))
    depth = jnp.arange(cells_z, dtype=jnp.int32).astype(jnp.float32) + 0.5 - 0.5 * cells_z
    coord_z = jnp.broadcast_to(depth[None, None, :], (slots, TY, cells_z))
    return jnp.stack([coord_x, coord_y, coord_z]).reshape(3, slots, TY * cells_z)

def closest(cell_list, points, nearest_sq):

    def one_slot(slot_pair):
        slot_cells, best_now = slot_pair
        step_x = slot_cells[0][:, None] - points[0][None, :]
        step_y = slot_cells[1][:, None] - points[1][None, :]
        step_z = slot_cells[2][:, None] - points[2][None, :]
        squared = step_x * step_x + step_y * step_y + step_z * step_z
        return jnp.minimum(best_now, lax.optimization_barrier(jnp.min(squared, axis=1)))
    return lax.map(one_slot, (jnp.moveaxis(cell_list, 1, 0), nearest_sq))

def place_tiles(tile_list, values, cells_x, cells_y, cells_z):
    tile_count = cells_x * (cells_y // TY)
    tile_grid = jnp.full((tile_count, TY * cells_z), dist_cap, jnp.float32)
    target = jnp.where(tile_list >= 0, tile_list, tile_count)
    tile_grid = tile_grid.at[target].set(values, mode='drop')
    return tile_grid.reshape(cells_x, cells_y, cells_z)

def neighbour(padded, direction, offset, interior):
    slices = [slice(None)]
    for dimension in range(3):
        begin = 2 + (offset if dimension == direction else 0)
        slices.append(slice(begin, begin + interior[dimension]))
    return padded[tuple(slices)]

def advance(padded, wall_dist, fluid_cells):
    interior = (padded.shape[1] - 4, padded.shape[2] - 4, padded.shape[3] - 4)
    center = neighbour(padded, 0, 0, interior)
    gradient = []
    laplace = jnp.zeros_like(center)
    for direction in range(3):
        plus_one = neighbour(padded, direction, 1, interior)
        minus_one = neighbour(padded, direction, -1, interior)
        plus_two = neighbour(padded, direction, 2, interior)
        minus_two = neighbour(padded, direction, -2, interior)
        gradient.append((minus_two - plus_two + 8.0 * (plus_one - minus_one)) / 12.0)
        laplace = laplace + (plus_one + minus_one - 2.0 * center)
    moving = center[:3]
    working = center[3]
    curl_x = gradient[1][2] - gradient[2][1]
    curl_y = gradient[2][0] - gradient[0][2]
    curl_z = gradient[0][1] - gradient[1][0]
    vort_rate = jnp.maximum(jnp.sqrt(curl_x * curl_x + curl_y * curl_y + curl_z * curl_z), floor_rate)
    positive = jnp.maximum(working, 0.0)
    chi_ratio = positive / viscosity
    chi_cubed = chi_ratio * chi_ratio * chi_ratio
    eddy_visc = positive * chi_cubed / (chi_cubed + visc_coef ** 3)
    diffusion = viscosity + eddy_visc
    shield_arg = diffusion / (vort_rate * karman * karman * wall_dist * wall_dist)
    shield = 1.0 - jnp.tanh((8.0 * shield_arg) ** 3)
    length = wall_dist - shield * jnp.maximum(wall_dist - des_coef, 0.0)
    convect = moving[0] * gradient[0] + moving[1] * gradient[1] + moving[2] * gradient[2]
    grad_sq = gradient[0][3] * gradient[0][3] + gradient[1][3] * gradient[1][3] + gradient[2][3] * gradient[2][3]
    nu_rhs = -convect[3] + sigma_inv * ((viscosity + positive) * laplace[3] + grad_coef * grad_sq) + prod_coef * vort_rate * working - wall_coef * working * jnp.abs(working) / (length * length)
    vel_rhs = -convect[:3] + diffusion[None] * laplace[:3]
    fluid_mask = fluid_cells.astype(jnp.float32)
    new_velocity = moving + time_step * fluid_mask[None] * vel_rhs
    new_nu = working + time_step * fluid_mask * nu_rhs
    return (new_velocity, new_nu)

def fill_ghosts(fields, send_rows, ghost_src, ghost_weight, ghost_cell):
    blocks = to_blocks(fields)
    live_rows = send_rows >= 0
    safe_rows = jnp.where(live_rows, send_rows, 0)

    def pick(block_state, row_list, live_mask):
        return jnp.where(live_mask[None], block_state[:, row_list], 0.0)
    outgoing = jax.vmap(jax.vmap(jax.vmap(pick)))(blocks, safe_rows, live_rows)
    outgoing = outgoing.reshape(N_GX, N_GY, N_GZ, 4, N_GX, N_GZ, CAP)
    incoming = outgoing.transpose(4, 1, 5, 3, 0, 2, 6).reshape(N_GX, N_GY, N_GZ, 4, PEERS * CAP)

    def interpolate(block_state, buffer, sources, weights, cell_list):
        values = buffer[:, sources]
        ghost_value = -lax.optimization_barrier(jnp.sum(weights[None] * values, axis=1))
        return block_state.at[:, cell_list].set(ghost_value)
    filled = jax.vmap(jax.vmap(jax.vmap(interpolate)))(blocks, incoming, ghost_src, ghost_weight, ghost_cell)
    return from_blocks(filled)

def wall_field(surface, pitch_angle, near_tiles):

    def one_device(device_id):
        col_x = device_id // (N_GY * N_GZ)
        span_index = device_id // N_GZ % N_GY
        col_z = device_id % N_GZ
        points = rotate(surface[col_x, col_z], pitch_angle)
        tile_list = near_tiles[col_x, span_index, col_z]
        cell_list = cell_coords(tile_list, span_index * CY, NY, CX, CY, CZ)
        initial = jnp.full((tile_list.shape[0], TY * CZ), jnp.inf, jnp.float32)
        nearest_sq = closest(cell_list, points, initial)
        distance = jnp.minimum(jnp.sqrt(nearest_sq + dist_eps), dist_cap)
        return place_tiles(tile_list, distance, CX, CY, CZ).reshape(1, CX * CY * CZ)
    blocks = lax.map(one_device, jnp.arange(N_GX * N_GY * N_GZ, dtype=jnp.int32))
    return from_blocks(blocks.reshape(N_GX, N_GY, N_GZ, 1, CX * CY * CZ))[0]

def reference(velocity, nu_tilde, fluid_cells, surface, pitch_angle, near_tiles, send_rows, ghost_cell, ghost_src, ghost_weight):
    fields = jnp.concatenate([velocity, nu_tilde[None]], axis=0)
    filled = fill_ghosts(fields, send_rows, ghost_src, ghost_weight, ghost_cell)
    wall_distance = wall_field(surface, pitch_angle, near_tiles)
    padded = jnp.pad(filled, ((0, 0), (2, 2), (2, 2), (2, 2)))
    new_velocity, new_nu_tilde = advance(padded, wall_distance, fluid_cells)
    return (new_velocity, new_nu_tilde, wall_distance)
```

```python
import jax
import jax.numpy as jnp
from jax import lax
from jax.experimental import pallas as pl
from jax.experimental.pallas import tpu as pltpu
from jax.sharding import PartitionSpec as P

f32 = jnp.float32
bf16 = jnp.bfloat16
i32 = jnp.int32

CX, CY, CZ = 8, 32, 128
ROWS = CX * CY
TY = 8

viscosity = 0.2
prod_coef = 0.1355
grad_coef = 0.622
sigma_inv = 1.5
karman = 0.41
visc_coef = 7.1
wall_coef = prod_coef / (karman * karman) + (1.0 + grad_coef) * sigma_inv
des_coef = 0.65
floor_rate = 0.3
dist_eps = 0.25
dist_cap = 8.0
time_step = 0.05

VMEM_LIMIT = 48 * 1024 * 1024


def in_two(values):
    high = values.astype(bf16)
    return high, (values - high.astype(f32)).astype(bf16)


def one_hot(index, count):
    level = lax.broadcasted_iota(i32, (count, index.shape[1]), 0)
    return jnp.where(level == index, 1.0, 0.0).astype(bf16)


def pick_group(values, index):
    groups = values.shape[0]
    bit = 0
    while groups > 1:
        groups //= 2
        mask = ((index >> bit) & 1) == 1
        pairs = values.reshape((groups, 2) + values.shape[1:])
        values = jnp.where(mask[None], pairs[:, 1], pairs[:, 0])
        bit += 1
    return values[0]


def two_rows(ref, pair):
    return jnp.concatenate([ref[pl.ds(2 * pair, 1), :], ref[pl.ds(2 * pair + 1, 1), :]], axis=1)


def pack_kernel(vel_ref, nu_ref, rows_ref, out_ref, turn_ref, table_ref):
    for f in range(4):
        block = vel_ref[f] if f < 3 else nu_ref[...]
        for half in range(2):
            turn_ref[half, pl.ds(f, CZ, stride=4), :] = block[half * 128:half * 128 + 128].T
    for half in range(2):
        high, low = in_two(turn_ref[half])
        table_ref[:, half * 128:half * 128 + 128] = high
        table_ref[:, ROWS + half * 128:ROWS + half * 128 + 128] = low
    top = lax.broadcasted_iota(i32, (8, 128), 0) < 4

    def step(pair, carry):
        rows = two_rows(rows_ref, pair)
        hot = one_hot(rows >> 7, ROWS)
        found = jnp.dot(
            table_ref[...], jnp.concatenate([hot, hot], axis=0), preferred_element_type=f32
        )
        column = rows & 127
        both = pick_group(found.reshape(CZ // 2, 8, 256), column >> 1)
        swapped = jnp.concatenate([both[4:], both[:4]], axis=0)
        odd = (column & 1) == 1
        first = jnp.where(odd[:, :128], swapped[:, :128], both[:, :128])
        second = jnp.where(odd[:, 128:], both[:, 128:], swapped[:, 128:])
        out_ref[pl.ds(pl.multiple_of(pair * 8, 8), 8), :] = jnp.where(top, first, second)
        return carry

    lax.fori_loop(0, rows_ref.shape[0] // 2, step, 0, unroll=4)


def prepare_kernel(
    tiles_ref, place_ref, pitch_ref, s0_ref, s1_ref, s2_ref, s3_ref, vel_ref, nu_ref, cell_ref,
    base_ref, wall_ref, hot_ref, low_ref, depth_ref, span_ref
):
    for pair in range(8):
        cell = two_rows(cell_ref, pair)
        hot_ref[:, pair * 256:(pair + 1) * 256] = one_hot(cell >> 7, ROWS)
        low_ref[:, pair * 256:(pair + 1) * 256] = one_hot(cell & 127, CZ)
    count = lax.dot_general(
        hot_ref[...], low_ref[...], (((1,), (1,)), ((), ())), preferred_element_type=f32
    )
    ghost = count > 0.5
    for f in range(4):
        block = vel_ref[f] if f < 3 else nu_ref[...]
        base_ref[f] = jnp.where(ghost, 0.0, block)

    angle = jnp.full((1, 128), pitch_ref[0], f32)
    cosine = jnp.cos(angle)
    sine = jnp.sin(angle)
    turned = []
    for ref in (s0_ref, s1_ref, s2_ref, s3_ref):
        x, y, z = ref[0:1, :], ref[1:2, :], ref[2:3, :]
        turned.append((cosine * x + sine * z, y, cosine * z - sine * x))
    depth = lax.broadcasted_iota(i32, (CZ, 128), 0).astype(f32) + (0.5 - 0.5 * CZ)
    for q in range(4):
        step_z = depth - turned[q][2]
        depth_ref[q] = step_z * step_z
    wall_ref[...] = jnp.full(wall_ref.shape, dist_cap, f32)
    start = place_ref[1] * CY
    for slot in range(8):
        tile = tiles_ref[slot]

        @pl.when(tile >= 0)
        def _():
            coord_x = (tile // 4).astype(f32) + (0.5 - 0.5 * CX)
            first = (tile % 4) * TY + start
            row = lax.broadcasted_iota(i32, (8, 128), 0) + first
            coord_y = row.astype(f32) + (0.5 - 0.5 * 4 * CY)
            for q in range(4):
                step_x = coord_x - turned[q][0]
                step_y = coord_y - turned[q][1]
                span_ref[q] = step_x * step_x + step_y * step_y
            rows = []
            for r in range(8):
                least = None
                for q in range(4):
                    here = span_ref[q, r:r + 1, :] + depth_ref[q]
                    least = here if least is None else jnp.minimum(least, here)
                rows.append(jnp.min(least.T, axis=0, keepdims=True))
            nearest = jnp.concatenate(rows, axis=0)
            wall_ref[tile] = jnp.minimum(jnp.sqrt(nearest + dist_eps), dist_cap)


def fill_kernel(
    inc_ref, src_ref, weight_ref, cell_ref, base_ref,
    filled_ref, xlo_ref, xhi_ref, ylo_ref, yhi_ref, zlo_ref, zhi_ref,
    table_ref, hot_ref, value_ref, flat_ref
):
    high, low = in_two(inc_ref[...])
    table_ref[:, :CZ] = high
    table_ref[:, CZ:] = low

    def step(block, carry):
        at = pl.ds(pl.multiple_of(block * 256, 256), 256)
        total = jnp.zeros((4, 256), f32)
        for t in range(8):
            source = src_ref[t:t + 1, at]
            hot = one_hot(source & 127, CZ)
            found = jnp.dot(
                table_ref[...], jnp.concatenate([hot, hot], axis=0), preferred_element_type=f32
            )
            peer = source >> 7
            both = pick_group(found.reshape(32, 8, 256), peer >> 1)
            value = jnp.where((peer & 1) == 1, both[4:], both[:4])
            total = total + weight_ref[t:t + 1, at] * value
        total = -total
        cell = two_rows(cell_ref, block)
        hot = one_hot(cell >> 7, ROWS)
        put = pl.multiple_of(block * 512, 512)
        hot_ref[:, pl.ds(put, 256)] = hot
        hot_ref[:, pl.ds(put + 256, 256)] = hot
        here = lax.broadcasted_iota(i32, (CZ, 256), 0) == (cell & 127)
        rest = total - total.astype(bf16).astype(f32)
        for f in range(4):
            value_ref[pl.ds(f * CZ, CZ), pl.ds(put, 256)] = jnp.where(
                here, total[f:f + 1], 0.0).astype(bf16)
            value_ref[pl.ds(f * CZ, CZ), pl.ds(put + 256, 256)] = jnp.where(
                here, rest[f:f + 1], 0.0).astype(bf16)
        return carry

    lax.fori_loop(0, 8, step, 0)
    added = lax.dot_general(
        hot_ref[...], value_ref[...], (((1,), (1,)), ((), ())), preferred_element_type=f32
    )
    for f in range(4):
        block = base_ref[f] + added[:, f * CZ:(f + 1) * CZ]
        filled_ref[f] = block
        flat_ref[pl.ds(f * ROWS, ROWS), :] = block
        xlo_ref[pl.ds(f * 64, 64), :] = block[:64]
        xhi_ref[pl.ds(f * 64, 64), :] = block[ROWS - 64:]
    for h in range(2):
        ylo_ref[pl.ds(h * 32, 32), :] = flat_ref[pl.ds(h, 32, stride=32), :]
        yhi_ref[pl.ds(h * 32, 32), :] = flat_ref[pl.ds(30 + h, 32, stride=32), :]
    for b in range(8):
        turn = flat_ref[pl.ds(b * 128, 128), :].T
        zlo_ref[pl.ds(b * 2, 2), :] = turn[0:2]
        zhi_ref[pl.ds(b * 2, 2), :] = turn[126:128]


def advance_kernel(
    place_ref, filled_ref, xlo_ref, xhi_ref, ylo_ref, yhi_ref, zlo_ref, zhi_ref, wall_ref, fluid_ref,
    vel_ref, nu_ref, pad_ref, edge_ref
):
    ix, iy, iz = place_ref[0], place_ref[1], place_ref[2]
    keep = lambda flag, value: jnp.where(flag, value, 0.0)
    for f in range(4):
        pad_ref[f, 2:10, 8:40, :] = filled_ref[f].reshape(8, 32, 128)
        pad_ref[f, 0:2, 8:40, :] = keep(ix > 0, xlo_ref[f * 64:(f + 1) * 64, :]).reshape(2, 32, 128)
        pad_ref[f, 10:12, 8:40, :] = keep(ix < 15, xhi_ref[f * 64:(f + 1) * 64, :]).reshape(2, 32, 128)
    for h in range(2):
        low = keep(iy > 0, ylo_ref[h * 32:(h + 1) * 32, :])
        high = keep(iy < 3, yhi_ref[h * 32:(h + 1) * 32, :])
        for f in range(4):
            for i in range(8):
                n = f * 8 + i
                pad_ref[f, 2 + i, 6 + h:7 + h, :] = low[n:n + 1]
                pad_ref[f, 2 + i, 40 + h:41 + h, :] = high[n:n + 1]
    zlow = keep(iz > 0, zlo_ref[...])
    zhigh = keep(iz < 3, zhi_ref[...])
    for b in range(8):
        block = jnp.concatenate(
            [zhigh[2 * b:2 * b + 2], jnp.zeros((124, 128), f32), zlow[2 * b:2 * b + 2]], axis=0
        )
        edge_ref[b // 2, (b % 2) * 4:(b % 2) * 4 + 4] = block.T.reshape(4, 32, 128)

    lane = lax.broadcasted_iota(i32, (8, 128), 1)

    def plane(i, carry):
        for c in range(4):
            j = 8 + 8 * c
            center, grads, laps = [], [], []
            for f in range(4):
                mid = pad_ref[f, i + 2, j:j + 8, :]
                edge = edge_ref[f, i, 8 * c:8 * c + 8, :]
                xs = [pad_ref[f, i + 2 + h, j:j + 8, :] for h in (-2, -1, 1, 2)]
                ys = [pad_ref[f, i + 2, j + h:j + 8 + h, :] for h in (-2, -1, 1, 2)]
                zs = [
                    pltpu.roll(jnp.where(lane >= 126, edge, mid), 2, 1),
                    pltpu.roll(jnp.where(lane >= 127, edge, mid), 1, 1),
                    pltpu.roll(jnp.where(lane < 1, edge, mid), 127, 1),
                    pltpu.roll(jnp.where(lane < 2, edge, mid), 126, 1),
                ]
                center.append(mid)
                grads.append([
                    ((m2 - p2) + 8.0 * (p1 - m1)) * (1.0 / 12.0) for m2, m1, p1, p2 in (xs, ys, zs)
                ])
                around = (xs[1] + xs[2]) + (ys[1] + ys[2]) + (zs[1] + zs[2])
                laps.append(around - 6.0 * mid)
            u, v, w, working = center
            curl_x = grads[2][1] - grads[1][2]
            curl_y = grads[0][2] - grads[2][0]
            curl_z = grads[1][0] - grads[0][1]
            rate = jnp.maximum(
                jnp.sqrt(curl_x * curl_x + curl_y * curl_y + curl_z * curl_z), floor_rate
            )
            positive = jnp.maximum(working, 0.0)
            chi = positive * (1.0 / viscosity)
            cubed = chi * chi * chi
            diffusion = viscosity + positive * cubed / (cubed + visc_coef**3)
            wall = wall_ref[i, 8 * c:8 * c + 8, :]
            arg = 8.0 * (diffusion / (rate * (karman * karman) * wall * wall))
            shield = 1.0 - jnp.tanh(arg * arg * arg)
            length = wall - shield * jnp.maximum(wall - des_coef, 0.0)
            convect = [u * g[0] + v * g[1] + w * g[2] for g in grads]
            gn = grads[3]
            grad_sq = gn[0] * gn[0] + gn[1] * gn[1] + gn[2] * gn[2]
            nu_rhs = (
                sigma_inv * ((viscosity + positive) * laps[3] + grad_coef * grad_sq)
                - convect[3]
                + prod_coef * rate * working
                - wall_coef * working * jnp.abs(working) / (length * length)
            )
            mask = fluid_ref[i, 8 * c:8 * c + 8, :].astype(f32) * time_step
            for f in range(3):
                vel_ref[f, i, 8 * c:8 * c + 8, :] = center[f] + mask * (diffusion * laps[f] - convect[f])
            nu_ref[i, 8 * c:8 * c + 8, :] = working + mask * nu_rhs
        return carry

    lax.fori_loop(0, 8, plane, 0)


def vmem():
    return pl.BlockSpec(memory_space=pltpu.VMEM)


def smem():
    return pl.BlockSpec(memory_space=pltpu.SMEM)


def call(kernel, out_shape, in_specs, scratch, name, flops, moved):
    many = isinstance(out_shape, (list, tuple))
    return pl.pallas_call(
        kernel,
        out_shape=out_shape,
        in_specs=in_specs,
        out_specs=[vmem()] * len(out_shape) if many else vmem(),
        scratch_shapes=scratch,
        compiler_params=pltpu.CompilerParams(vmem_limit_bytes=VMEM_LIMIT),
        cost_estimate=pl.CostEstimate(flops=flops, bytes_accessed=moved, transcendentals=0),
        name=name,
    )


def ring(block, axis, shift):
    count = lax.axis_size(axis)
    return lax.ppermute(block, axis, [(i, (i + shift) % count) for i in range(count)])


def on_device(
    velocity, nu_tilde, fluid_cells, surface, pitch_angle, near_tiles, send_rows, ghost_cell,
    ghost_src, ghost_weight,
):
    shape = lambda *dims, dtype=f32: jax.ShapeDtypeStruct(dims, dtype)
    vel = velocity.reshape(3, ROWS, CZ)
    nu = nu_tilde.reshape(ROWS, CZ)
    cells = ghost_cell.reshape(16, 128)
    place = jnp.stack([lax.axis_index("gx"), lax.axis_index("gy"), lax.axis_index("gz")]).astype(i32)
    own = surface.reshape(3, 128)
    others = [ring(own, "gy", d) for d in (1, 2, 3)]

    outgoing = call(
        pack_kernel, shape(256, 128), [vmem()] * 3,
        [pltpu.VMEM((2, 512, 128), f32), pltpu.VMEM((512, 2 * ROWS), bf16)],
        "pack_rows", 4_000_000_000, 1_000_000,
    )(vel, nu, send_rows.reshape(64, 128))
    incoming = lax.all_to_all(
        outgoing.reshape(256 * 128), ("gx", "gz"), split_axis=0, concat_axis=0, tiled=True
    ).reshape(256, 128)

    base, wall = call(
        prepare_kernel, (shape(4, ROWS, CZ), shape(32, TY, CZ)),
        [smem()] * 3 + [vmem()] * 7,
        [pltpu.VMEM((ROWS, 2048), bf16), pltpu.VMEM((CZ, 2048), bf16),
         pltpu.VMEM((4, CZ, 128), f32), pltpu.VMEM((4, 8, 128), f32)],
        "prepare", 200_000_000, 2_000_000,
    )(near_tiles.reshape(8), place, pitch_angle, own, *others, vel, nu, cells)

    filled, xlo, xhi, ylo, yhi, zlo, zhi = call(
        fill_kernel,
        (shape(4, ROWS, CZ), shape(256, 128), shape(256, 128), shape(64, 128), shape(64, 128),
         shape(16, 128), shape(16, 128)),
        [vmem()] * 5,
        [pltpu.VMEM((256, 256), bf16), pltpu.VMEM((ROWS, 4096), bf16),
         pltpu.VMEM((512, 4096), bf16), pltpu.VMEM((4 * ROWS, CZ), f32)],
        "fill_ghosts", 4_000_000_000, 2_000_000,
    )(incoming, ghost_src.reshape(8, 2048), ghost_weight.reshape(8, 2048), cells, base)

    from_below = [ring(xhi, "gx", 1), ring(yhi, "gy", 1), ring(zhi, "gz", 1)]
    from_above = [ring(xlo, "gx", -1), ring(ylo, "gy", -1), ring(zlo, "gz", -1)]
    wall = wall.reshape(CX, CY, CZ)
    new_velocity, new_nu = call(
        advance_kernel, (shape(3, CX, CY, CZ), shape(CX, CY, CZ)),
        [smem()] + [vmem()] * 9,
        [pltpu.VMEM((4, 12, 48, CZ), f32), pltpu.VMEM((4, CX, CY, CZ), f32)],
        "advance", 20_000_000, 3_000_000,
    )(place, filled, from_below[0], from_above[0], from_below[1], from_above[1],
      from_below[2], from_above[2], wall, fluid_cells)
    return new_velocity, new_nu, wall


def solution(mesh):
    in_specs = (
        P(None, "gx", "gy", "gz"),
        P("gx", "gy", "gz"),
        P("gx", "gy", "gz"),
        P("gx", "gz", None, "gy"),
        P(),
        P("gx", "gy", "gz", None),
        P("gx", "gy", "gz", None, None),
        P("gx", "gy", "gz", None),
        P("gx", "gy", "gz", None, None),
        P("gx", "gy", "gz", None, None),
    )
    out_specs = (P(None, "gx", "gy", "gz"), P("gx", "gy", "gz"), P("gx", "gy", "gz"))
    return jax.shard_map(
        on_device, mesh=mesh, in_specs=in_specs, out_specs=out_specs, check_vma=False
    )
```

```python
import jax
import jax.numpy as jnp
from jax import lax
from jax.experimental import pallas as pl
from jax.experimental.pallas import tpu as pltpu
from jax.sharding import PartitionSpec as P

f32 = jnp.float32
bf16 = jnp.bfloat16
i32 = jnp.int32

CX, CY, CZ = 8, 32, 128
ROWS = CX * CY
TY = 8

viscosity = 0.2
prod_coef = 0.1355
grad_coef = 0.622
sigma_inv = 1.5
karman = 0.41
visc_coef = 7.1
wall_coef = prod_coef / (karman * karman) + (1.0 + grad_coef) * sigma_inv
des_coef = 0.65
floor_rate = 0.3
dist_eps = 0.25
dist_cap = 8.0
time_step = 0.05

VMEM_LIMIT = 48 * 1024 * 1024


def in_two(values):
    high = values.astype(bf16)
    return high, (values - high.astype(f32)).astype(bf16)


def one_hot(index, count):
    level = lax.broadcasted_iota(i32, (count, index.shape[1]), 0)
    return jnp.where(level == index, 1.0, 0.0).astype(bf16)


def pick_group(values, index):
    groups = values.shape[0]
    bit = 0
    while groups > 1:
        groups //= 2
        mask = ((index >> bit) & 1) == 1
        pairs = values.reshape((groups, 2) + values.shape[1:])
        values = jnp.where(mask[None], pairs[:, 1], pairs[:, 0])
        bit += 1
    return values[0]


def two_rows(ref, pair):
    return jnp.concatenate([ref[pl.ds(2 * pair, 1), :], ref[pl.ds(2 * pair + 1, 1), :]], axis=1)


def pack_kernel(
    vel_hbm, nu_hbm, rows_hbm, out_ref, table_ref, vel_ref, nu_ref, rows_ref, turn_ref, sems
):
    copies = [
        pltpu.make_async_copy(vel_hbm, vel_ref, sems.at[0]),
        pltpu.make_async_copy(nu_hbm, nu_ref, sems.at[1]),
        pltpu.make_async_copy(rows_hbm, rows_ref, sems.at[2]),
    ]
    for copy in copies:
        copy.start()
    copies[0].wait()
    for f in range(4):
        if f == 3:
            copies[1].wait()
        block = vel_ref[f] if f < 3 else nu_ref[...]
        for half in range(2):
            turn_ref[half, pl.ds(f, CZ, stride=4), :] = block[half * 128:half * 128 + 128].T
    for half in range(2):
        high, low = in_two(turn_ref[half])
        table_ref[:, half * 128:half * 128 + 128] = high
        table_ref[:, ROWS + half * 128:ROWS + half * 128 + 128] = low
    copies[2].wait()
    top = lax.broadcasted_iota(i32, (8, 128), 0) < 4

    def step(pair, carry):
        rows = two_rows(rows_ref, pair)
        hot = one_hot(rows >> 7, ROWS)
        found = jnp.dot(
            table_ref[...], jnp.concatenate([hot, hot], axis=0), preferred_element_type=f32
        )
        column = rows & 127
        both = pick_group(found.reshape(CZ // 2, 8, 256), column >> 1)
        swapped = jnp.concatenate([both[4:], both[:4]], axis=0)
        odd = (column & 1) == 1
        first = jnp.where(odd[:, :128], swapped[:, :128], both[:, :128])
        second = jnp.where(odd[:, 128:], both[:, 128:], swapped[:, 128:])
        out_ref[pl.ds(pl.multiple_of(pair * 8, 8), 8), :] = jnp.where(top, first, second)
        return carry

    lax.fori_loop(0, 32, step, 0, unroll=4)


def prepare_kernel(vel_ref, nu_ref, cell_ref, base_ref, hot_ref, low_ref):
    for pair in range(8):
        cell = two_rows(cell_ref, pair)
        hot_ref[:, pair * 256:(pair + 1) * 256] = one_hot(cell >> 7, ROWS)
        low_ref[:, pair * 256:(pair + 1) * 256] = one_hot(cell & 127, CZ)
    count = lax.dot_general(
        hot_ref[...], low_ref[...], (((1,), (1,)), ((), ())), preferred_element_type=f32
    )
    ghost = count > 0.5
    for f in range(4):
        block = vel_ref[f] if f < 3 else nu_ref[...]
        base_ref[f] = jnp.where(ghost, 0.0, block)


def wall_kernel(
    tiles_ref, pitch_ref, near_ref, far_ref, wall_ref, depth_ref, span_ref
):
    angle = jnp.full((1, 128), pitch_ref[0], f32)
    cosine = jnp.cos(angle)
    sine = jnp.sin(angle)
    turned = []
    for ref, n in ((near_ref, 0), (near_ref, 3), (far_ref, 0), (far_ref, 3)):
        x, y, z = ref[n:n + 1, :], ref[n + 1:n + 2, :], ref[n + 2:n + 3, :]
        turned.append((cosine * x + sine * z, y, cosine * z - sine * x))
    depth = lax.broadcasted_iota(i32, (CZ, 128), 0).astype(f32) + (0.5 - 0.5 * CZ)
    for q in range(4):
        step_z = depth - turned[q][2]
        depth_ref[q] = step_z * step_z
    wall_ref[...] = jnp.full(wall_ref.shape, dist_cap, f32)
    start = lax.axis_index("gy") * CY
    for slot in range(8):
        tile = tiles_ref[slot]

        @pl.when(tile >= 0)
        def _():
            coord_x = (tile // 4).astype(f32) + (0.5 - 0.5 * CX)
            first = (tile % 4) * TY + start
            row = lax.broadcasted_iota(i32, (8, 128), 0) + first
            coord_y = row.astype(f32) + (0.5 - 0.5 * 4 * CY)
            for q in range(4):
                step_x = coord_x - turned[q][0]
                step_y = coord_y - turned[q][1]
                span_ref[q] = step_x * step_x + step_y * step_y
            rows = []
            for r in range(8):
                least = None
                for q in range(4):
                    here = span_ref[q, r:r + 1, :] + depth_ref[q]
                    least = here if least is None else jnp.minimum(least, here)
                rows.append(jnp.min(least.T, axis=0, keepdims=True))
            nearest = jnp.concatenate(rows, axis=0)
            wall_ref[tile] = jnp.minimum(jnp.sqrt(nearest + dist_eps), dist_cap)


def fill_kernel(
    inc_ref, src_ref, weight_ref, cell_ref, base_ref,
    filled_ref, x1_ref, x2_ref, y1_ref, y2_ref, z1_ref, z2_ref,
    table_ref, hot_ref, value_ref, flat_ref
):
    high, low = in_two(inc_ref[...])
    table_ref[:, :CZ] = high
    table_ref[:, CZ:] = low

    def step(block, carry):
        at = pl.ds(pl.multiple_of(block * 256, 256), 256)
        total = jnp.zeros((4, 256), f32)
        for t in range(8):
            source = src_ref[t:t + 1, at]
            hot = one_hot(source & 127, CZ)
            found = jnp.dot(
                table_ref[...], jnp.concatenate([hot, hot], axis=0), preferred_element_type=f32
            )
            peer = source >> 7
            both = pick_group(found.reshape(32, 8, 256), peer >> 1)
            value = jnp.where((peer & 1) == 1, both[4:], both[:4])
            total = total + weight_ref[t:t + 1, at] * value
        total = -total
        cell = two_rows(cell_ref, block)
        hot = one_hot(cell >> 7, ROWS)
        put = pl.multiple_of(block * 512, 512)
        hot_ref[:, pl.ds(put, 256)] = hot
        hot_ref[:, pl.ds(put + 256, 256)] = hot
        here = lax.broadcasted_iota(i32, (CZ, 256), 0) == (cell & 127)
        rest = total - total.astype(bf16).astype(f32)
        for f in range(4):
            value_ref[pl.ds(f * CZ, CZ), pl.ds(put, 256)] = jnp.where(
                here, total[f:f + 1], 0.0).astype(bf16)
            value_ref[pl.ds(f * CZ, CZ), pl.ds(put + 256, 256)] = jnp.where(
                here, rest[f:f + 1], 0.0).astype(bf16)
        return carry

    lax.fori_loop(0, 8, step, 0)
    added = lax.dot_general(
        hot_ref[...], value_ref[...], (((1,), (1,)), ((), ())), preferred_element_type=f32
    )
    even_x, even_y, even_z = [(lax.axis_index(axis) & 1) == 0 for axis in ("gx", "gy", "gz")]
    for f in range(4):
        block = base_ref[f] + added[:, f * CZ:(f + 1) * CZ]
        filled_ref[f] = block
        flat_ref[pl.ds(f * ROWS, ROWS), :] = block
        low, high = block[:64], block[ROWS - 64:]
        x1_ref[pl.ds(f * 64, 64), :] = jnp.where(even_x, high, low)
        x2_ref[pl.ds(f * 64, 64), :] = jnp.where(even_x, low, high)
    for h in range(2):
        low = flat_ref[pl.ds(h, 32, stride=32), :]
        high = flat_ref[pl.ds(30 + h, 32, stride=32), :]
        y1_ref[pl.ds(h * 32, 32), :] = jnp.where(even_y, high, low)
        y2_ref[pl.ds(h * 32, 32), :] = jnp.where(even_y, low, high)
    for b in range(8):
        turn = flat_ref[pl.ds(b * 128, 128), :].T
        z1_ref[pl.ds(b * 2, 2), :] = jnp.where(even_z, turn[126:128], turn[0:2])
        z2_ref[pl.ds(b * 2, 2), :] = jnp.where(even_z, turn[0:2], turn[126:128])


def advance_kernel(
    filled_ref, x1_ref, x2_ref, y1_ref, y2_ref, z1_ref, z2_ref, wall_ref, fluid_ref,
    vel_ref, nu_ref, pad_ref, edge_ref
):
    ix, iy, iz = lax.axis_index("gx"), lax.axis_index("gy"), lax.axis_index("gz")

    def sides(index, last, first, second):
        odd = (index & 1) == 1
        below = jnp.where(odd, first, second)
        above = jnp.where(odd, second, first)
        return jnp.where(index > 0, below, 0.0), jnp.where(index < last, above, 0.0)

    for f in range(4):
        pad_ref[f, 2:10, 8:40, :] = filled_ref[f].reshape(8, 32, 128)
        at = pl.ds(f * 64, 64)
        below, above = sides(ix, 15, x1_ref[at, :], x2_ref[at, :])
        pad_ref[f, 0:2, 8:40, :] = below.reshape(2, 32, 128)
        pad_ref[f, 10:12, 8:40, :] = above.reshape(2, 32, 128)
    below, above = sides(iy, 3, y1_ref[...], y2_ref[...])
    for h in range(2):
        for f in range(4):
            for i in range(8):
                n = h * 32 + f * 8 + i
                pad_ref[f, 2 + i, 6 + h:7 + h, :] = below[n:n + 1]
                pad_ref[f, 2 + i, 40 + h:41 + h, :] = above[n:n + 1]
    below, above = sides(iz, 3, z1_ref[...], z2_ref[...])
    for b in range(8):
        block = jnp.concatenate(
            [above[2 * b:2 * b + 2], jnp.zeros((124, 128), f32), below[2 * b:2 * b + 2]], axis=0
        )
        edge_ref[b // 2, (b % 2) * 4:(b % 2) * 4 + 4] = block.T.reshape(4, 32, 128)

    lane = lax.broadcasted_iota(i32, (8, 128), 1)

    def plane(i, carry):
        for c in range(4):
            j = 8 + 8 * c
            center, grads, laps = [], [], []
            for f in range(4):
                mid = pad_ref[f, i + 2, j:j + 8, :]
                edge = edge_ref[f, i, 8 * c:8 * c + 8, :]
                xs = [pad_ref[f, i + 2 + h, j:j + 8, :] for h in (-2, -1, 1, 2)]
                ys = [pad_ref[f, i + 2, j + h:j + 8 + h, :] for h in (-2, -1, 1, 2)]
                zs = [
                    pltpu.roll(jnp.where(lane >= 126, edge, mid), 2, 1),
                    pltpu.roll(jnp.where(lane >= 127, edge, mid), 1, 1),
                    pltpu.roll(jnp.where(lane < 1, edge, mid), 127, 1),
                    pltpu.roll(jnp.where(lane < 2, edge, mid), 126, 1),
                ]
                center.append(mid)
                grads.append([
                    ((m2 - p2) + 8.0 * (p1 - m1)) * (1.0 / 12.0) for m2, m1, p1, p2 in (xs, ys, zs)
                ])
                around = (xs[1] + xs[2]) + (ys[1] + ys[2]) + (zs[1] + zs[2])
                laps.append(around - 6.0 * mid)
            u, v, w, working = center
            curl_x = grads[2][1] - grads[1][2]
            curl_y = grads[0][2] - grads[2][0]
            curl_z = grads[1][0] - grads[0][1]
            rate = jnp.maximum(
                jnp.sqrt(curl_x * curl_x + curl_y * curl_y + curl_z * curl_z), floor_rate
            )
            positive = jnp.maximum(working, 0.0)
            chi = positive * (1.0 / viscosity)
            cubed = chi * chi * chi
            diffusion = viscosity + positive * cubed / (cubed + visc_coef**3)
            wall = wall_ref[i, 8 * c:8 * c + 8, :]
            arg = 8.0 * (diffusion / (rate * (karman * karman) * wall * wall))
            shield = 1.0 - jnp.tanh(arg * arg * arg)
            length = wall - shield * jnp.maximum(wall - des_coef, 0.0)
            convect = [u * g[0] + v * g[1] + w * g[2] for g in grads]
            gn = grads[3]
            grad_sq = gn[0] * gn[0] + gn[1] * gn[1] + gn[2] * gn[2]
            nu_rhs = (
                sigma_inv * ((viscosity + positive) * laps[3] + grad_coef * grad_sq)
                - convect[3]
                + prod_coef * rate * working
                - wall_coef * working * jnp.abs(working) / (length * length)
            )
            mask = fluid_ref[i, 8 * c:8 * c + 8, :].astype(f32) * time_step
            for f in range(3):
                vel_ref[f, i, 8 * c:8 * c + 8, :] = center[f] + mask * (diffusion * laps[f] - convect[f])
            nu_ref[i, 8 * c:8 * c + 8, :] = working + mask * nu_rhs
        return carry

    lax.fori_loop(0, 8, plane, 0)


def vmem():
    return pl.BlockSpec(memory_space=pltpu.VMEM)


def anywhere():
    return pl.BlockSpec(memory_space=pl.ANY)


def smem():
    return pl.BlockSpec(memory_space=pltpu.SMEM)


def call(kernel, out_shape, in_specs, scratch, name, flops, moved, limit=VMEM_LIMIT):
    many = isinstance(out_shape, (list, tuple))
    return pl.pallas_call(
        kernel,
        out_shape=out_shape,
        in_specs=in_specs,
        out_specs=[vmem()] * len(out_shape) if many else vmem(),
        scratch_shapes=scratch,
        compiler_params=pltpu.CompilerParams(vmem_limit_bytes=limit),
        cost_estimate=pl.CostEstimate(flops=flops, bytes_accessed=moved, transcendentals=0),
        name=name,
    )


def exchange(block, axis, bit):
    count = lax.axis_size(axis)
    return lax.ppermute(block, axis, [(i, i ^ bit) for i in range(count)])


def swap_up(block, axis):
    return exchange(block, axis, 1)


def swap_down(block, axis):
    count = lax.axis_size(axis)
    return lax.ppermute(
        block, axis, [(i, (i + (1 if i % 2 else -1)) % count) for i in range(count)]
    )


def on_device(
    velocity, nu_tilde, fluid_cells, surface, pitch_angle, near_tiles, send_rows, ghost_cell,
    ghost_src, ghost_weight,
):
    shape = lambda *dims, dtype=f32: jax.ShapeDtypeStruct(dims, dtype)
    vel = velocity.reshape(3, ROWS, CZ)
    nu = nu_tilde.reshape(ROWS, CZ)
    cells = ghost_cell.reshape(16, 128)
    rows = send_rows.reshape(64, 128)
    points = surface.reshape(3, 128)
    points = jnp.concatenate([points, exchange(points, "gy", 1)])

    outgoing = call(
        pack_kernel, shape(256, 128), [anywhere()] * 3,
        [pltpu.VMEM((512, 2 * ROWS), bf16),
         pltpu.VMEM((3, ROWS, CZ), f32), pltpu.VMEM((ROWS, CZ), f32), pltpu.VMEM((64, 128), i32),
         pltpu.VMEM((2, 512, 128), f32), pltpu.SemaphoreType.DMA((3,))],
        "pack_rows", 4_000_000_000, 1_000_000, 60 * 1024 * 1024,
    )(vel, nu, rows)
    outgoing, points = lax.optimization_barrier((outgoing, points))
    incoming = lax.all_to_all(
        outgoing.reshape(256 * 128), ("gx", "gz"), split_axis=0, concat_axis=0, tiled=True
    ).reshape(256, 128)
    far_points = exchange(points, "gy", 2)

    base = call(
        prepare_kernel, shape(4, ROWS, CZ), [vmem()] * 3,
        [pltpu.VMEM((ROWS, 2048), bf16), pltpu.VMEM((CZ, 2048), bf16)],
        "prepare", 200_000_000, 2_000_000,
    )(vel, nu, cells)

    wall = call(
        wall_kernel, shape(32, TY, CZ), [smem()] * 2 + [vmem()] * 2,
        [pltpu.VMEM((4, CZ, 128), f32), pltpu.VMEM((4, 8, 128), f32)],
        "wall", 30_000_000, 200_000,
    )(near_tiles.reshape(8), pitch_angle, points, far_points)

    base, wall = lax.optimization_barrier((base, wall))
    filled, x1, x2, y1, y2, z1, z2 = call(
        fill_kernel,
        (shape(4, ROWS, CZ), shape(256, 128), shape(256, 128), shape(64, 128), shape(64, 128),
         shape(16, 128), shape(16, 128)),
        [vmem()] * 5,
        [pltpu.VMEM((256, 256), bf16), pltpu.VMEM((ROWS, 4096), bf16),
         pltpu.VMEM((512, 4096), bf16), pltpu.VMEM((4 * ROWS, CZ), f32)],
        "fill_ghosts", 4_000_000_000, 2_000_000,
    )(incoming, ghost_src.reshape(8, 2048), ghost_weight.reshape(8, 2048), cells, base)

    x1, x2 = swap_up(x1, "gx"), swap_down(x2, "gx")
    y1, y2 = swap_up(y1, "gy"), swap_down(y2, "gy")
    z1 = swap_up(z1, "gz")
    z2, x1 = lax.optimization_barrier((z2, x1))
    z2 = swap_down(z2, "gz")

    wall = wall.reshape(CX, CY, CZ)
    new_velocity, new_nu = call(
        advance_kernel, (shape(3, CX, CY, CZ), shape(CX, CY, CZ)), [vmem()] * 9,
        [pltpu.VMEM((4, 12, 48, CZ), f32), pltpu.VMEM((4, CX, CY, CZ), f32)],
        "advance", 20_000_000, 3_000_000,
    )(filled, x1, x2, y1, y2, z1, z2, wall, fluid_cells)
    return new_velocity, new_nu, wall


def solution(mesh):
    in_specs = (
        P(None, "gx", "gy", "gz"),
        P("gx", "gy", "gz"),
        P("gx", "gy", "gz"),
        P("gx", "gz", None, "gy"),
        P(),
        P("gx", "gy", "gz", None),
        P("gx", "gy", "gz", None, None),
        P("gx", "gy", "gz", None),
        P("gx", "gy", "gz", None, None),
        P("gx", "gy", "gz", None, None),
    )
    out_specs = (P(None, "gx", "gy", "gz"), P("gx", "gy", "gz"), P("gx", "gy", "gz"))
    return jax.shard_map(
        on_device, mesh=mesh, in_specs=in_specs, out_specs=out_specs, check_vma=False
    )
```

```python
import jax
import jax.numpy as jnp
from jax import lax
from jax.experimental import pallas as pl
from jax.experimental.pallas import tpu as pltpu
from jax.sharding import PartitionSpec as P

f32 = jnp.float32
bf16 = jnp.bfloat16
i32 = jnp.int32

CX, CY, CZ = 8, 32, 128
ROWS = CX * CY
TY = 8

viscosity = 0.2
prod_coef = 0.1355
grad_coef = 0.622
sigma_inv = 1.5
karman = 0.41
visc_coef = 7.1
wall_coef = prod_coef / (karman * karman) + (1.0 + grad_coef) * sigma_inv
des_coef = 0.65
floor_rate = 0.3
dist_eps = 0.25
dist_cap = 8.0
time_step = 0.05

VMEM_LIMIT = 24 * 1024 * 1024


def in_two(values):
    high = values.astype(bf16)
    return high, (values - high.astype(f32)).astype(bf16)


def one_hot(index, count):
    level = lax.broadcasted_iota(i32, (count, 1), 0).astype(f32).astype(bf16)
    return jnp.where(level == index.astype(f32).astype(bf16), jnp.ones((), bf16), jnp.zeros((), bf16))


def pick_group(values, index):
    groups = values.shape[0]
    bit = 0
    while groups > 1:
        groups //= 2
        mask = ((index >> bit) & 1) == 1
        pairs = values.reshape((groups, 2) + values.shape[1:])
        values = jnp.where(mask[None], pairs[:, 1], pairs[:, 0])
        bit += 1
    return values[0]


def two_rows(ref, pair):
    return jnp.concatenate([ref[pl.ds(2 * pair, 1), :], ref[pl.ds(2 * pair + 1, 1), :]], axis=1)


def pack_kernel(
    vel_hbm, nu_hbm, rows_hbm, out_ref, table_ref, vel_ref, nu_ref, rows_ref, turn_ref, sems
):
    copies = [
        pltpu.make_async_copy(vel_hbm, vel_ref, sems.at[0]),
        pltpu.make_async_copy(nu_hbm, nu_ref, sems.at[1]),
        pltpu.make_async_copy(rows_hbm, rows_ref, sems.at[2]),
    ]
    for copy in copies:
        copy.start()
    copies[0].wait()
    for f in range(4):
        if f == 3:
            copies[1].wait()
        block = vel_ref[f] if f < 3 else nu_ref[...]
        for half in range(2):
            turn_ref[half, pl.ds(f, CZ, stride=4), :] = block[half * 128:half * 128 + 128].T
    for half in range(2):
        high, low = in_two(turn_ref[half])
        table_ref[:, half * 128:half * 128 + 128] = high
        table_ref[:, ROWS + half * 128:ROWS + half * 128 + 128] = low
    copies[2].wait()
    top = lax.broadcasted_iota(i32, (8, 128), 0) < 4

    def step(pair, carry):
        rows = two_rows(rows_ref, pair)
        hot = one_hot(rows >> 7, ROWS)
        found = jnp.dot(
            table_ref[...], jnp.concatenate([hot, hot], axis=0), preferred_element_type=f32
        )
        column = rows & 127
        both = pick_group(found.reshape(CZ // 2, 8, 256), column >> 1)
        swapped = jnp.concatenate([both[4:], both[:4]], axis=0)
        odd = (column & 1) == 1
        first = jnp.where(odd[:, :128], swapped[:, :128], both[:, :128])
        second = jnp.where(odd[:, 128:], both[:, 128:], swapped[:, 128:])
        out_ref[pl.ds(pl.multiple_of(pair * 8, 8), 8), :] = jnp.where(top, first, second)
        return carry

    lax.fori_loop(0, 32, step, 0, unroll=32)


def prepare_kernel(vel_ref, nu_ref, cell_ref, base_ref, hot_ref, low_ref):
    for pair in range(8):
        cell = two_rows(cell_ref, pair)
        hot_ref[:, pair * 256:(pair + 1) * 256] = one_hot(cell >> 7, ROWS)
        low_ref[:, pair * 256:(pair + 1) * 256] = one_hot(cell & 127, CZ)
    count = lax.dot_general(
        hot_ref[...], low_ref[...], (((1,), (1,)), ((), ())), preferred_element_type=f32
    )
    ghost = count > 0.5
    for f in range(4):
        block = vel_ref[f] if f < 3 else nu_ref[...]
        base_ref[f] = jnp.where(ghost, 0.0, block)


def turn_points(pitch_ref, near_ref, far_ref, depth_ref):
    angle = jnp.broadcast_to(pitch_ref[...], (1, 128))
    cosine = jnp.cos(angle)
    sine = jnp.sin(angle)
    depth = lax.broadcasted_iota(i32, (CZ, 128), 0).astype(f32) + (0.5 - 0.5 * CZ)
    turned = []
    for q, (ref, n) in enumerate(((near_ref, 0), (near_ref, 3), (far_ref, 0), (far_ref, 3))):
        x, y, z = ref[n], ref[n + 1], ref[n + 2]
        turned.append((cosine * x + sine * z, y))
        step_z = depth - (cosine * z - sine * x)
        depth_ref[q] = step_z * step_z
    return turned


def tile_at(tiles_ref, slot):
    return jnp.max(tiles_ref[:, slot:slot + 1].astype(f32)).astype(i32)


def tile_distance(tile, turned, depth_ref, span_ref):
    coord_x = (tile // 4).astype(f32) + (0.5 - 0.5 * CX)
    first = (tile % 4) * TY + lax.axis_index("gy") * CY
    coord_y = (lax.broadcasted_iota(i32, (8, 128), 0) + first).astype(f32) + (0.5 - 0.5 * 4 * CY)
    for q in range(4):
        step_x = coord_x - turned[q][0]
        step_y = coord_y - turned[q][1]
        span_ref[q] = step_x * step_x + step_y * step_y
    rows = []
    for r in range(8):
        least = None
        for q in range(4):
            here = span_ref[q, r:r + 1, :] + depth_ref[q]
            least = here if least is None else jnp.minimum(least, here)
        rows.append(jnp.min(least.T, axis=0, keepdims=True))
    return jnp.minimum(jnp.sqrt(jnp.concatenate(rows, axis=0) + dist_eps), dist_cap)


def wall_kernel(
    tiles_ref, pitch_ref, near_ref, far_ref, wall_ref, again_ref, depth_ref, span_ref
):
    tiles = [tile_at(tiles_ref, slot) for slot in range(8)]
    turned = turn_points(pitch_ref, near_ref, far_ref, depth_ref)
    wall_ref[...] = jnp.full(wall_ref.shape, dist_cap, f32)
    for slot in range(8):

        @pl.when(tiles[slot] >= 0)
        def _():
            wall_ref[tiles[slot]] = tile_distance(tiles[slot], turned, depth_ref, span_ref)

    again_ref[...] = wall_ref[...]


def fill_kernel(
    inc_ref, src_ref, weight_ref, base_ref, hot_ref, low_ref,
    filled_ref, x1_ref, x2_ref, y1_ref, y2_ref, z1_ref, z2_ref,
    table_ref, value_ref, flat_ref
):
    high, low = in_two(inc_ref[...])
    table_ref[:, :CZ] = high
    table_ref[:, CZ:] = low

    def step(block, carry):
        at = pl.ds(pl.multiple_of(block * 256, 256), 256)
        total = jnp.zeros((4, 256), f32)
        for t in range(8):
            source = src_ref[t:t + 1, at]
            hot = one_hot(source & 127, CZ)
            found = jnp.dot(
                table_ref[...], jnp.concatenate([hot, hot], axis=0), preferred_element_type=f32
            )
            peer = source >> 7
            both = pick_group(found.reshape(32, 8, 256), peer >> 1)
            value = jnp.where((peer & 1) == 1, both[4:], both[:4])
            total = total + weight_ref[t:t + 1, at] * value
        total = -total
        high = total.astype(bf16).astype(f32)
        rest = total - high
        low_hot = low_ref[:, at]
        for f in range(4):
            value_ref[pl.ds(f * CZ, CZ), at] = low_hot * high[f:f + 1].astype(bf16)
            value_ref[pl.ds((4 + f) * CZ, CZ), at] = low_hot * rest[f:f + 1].astype(bf16)
        return carry

    lax.fori_loop(0, 8, step, 0, unroll=8)
    added = lax.dot_general(
        hot_ref[...], value_ref[...], (((1,), (1,)), ((), ())), preferred_element_type=f32
    )
    added = added[:, :4 * CZ] + added[:, 4 * CZ:]
    even_x, even_y, even_z = [(lax.axis_index(axis) & 1) == 0 for axis in ("gx", "gy", "gz")]
    for f in range(4):
        block = base_ref[f] + added[:, f * CZ:(f + 1) * CZ]
        filled_ref[f] = block
        flat_ref[pl.ds(f * ROWS, ROWS), :] = block
        low, high = block[:64], block[ROWS - 64:]
        x1_ref[pl.ds(f * 64, 64), :] = jnp.where(even_x, high, low)
        x2_ref[pl.ds(f * 64, 64), :] = jnp.where(even_x, low, high)
    for h in range(2):
        low = flat_ref[pl.ds(h, 32, stride=32), :]
        high = flat_ref[pl.ds(30 + h, 32, stride=32), :]
        y1_ref[pl.ds(h * 32, 32), :] = jnp.where(even_y, high, low)
        y2_ref[pl.ds(h * 32, 32), :] = jnp.where(even_y, low, high)
    for b in range(8):
        turn = flat_ref[pl.ds(b * 128, 128), :].T
        z1_ref[pl.ds(b * 2, 2), :] = jnp.where(even_z, turn[126:128], turn[0:2])
        z2_ref[pl.ds(b * 2, 2), :] = jnp.where(even_z, turn[0:2], turn[126:128])


def advance_kernel(
    filled_ref, x1_ref, x2_ref, y1_ref, y2_ref, z1_ref, z2_ref, wall_ref, fluid_ref,
    vel_ref, nu_ref, pad_ref, edge_ref
):
    ix, iy, iz = lax.axis_index("gx"), lax.axis_index("gy"), lax.axis_index("gz")

    def sides(index, last, first, second):
        odd = (index & 1) == 1
        below = jnp.where(odd, first, second)
        above = jnp.where(odd, second, first)
        return jnp.where(index > 0, below, 0.0), jnp.where(index < last, above, 0.0)

    for f in range(4):
        pad_ref[f, 2:10, 8:40, :] = filled_ref[f].reshape(8, 32, 128)
        at = pl.ds(f * 64, 64)
        below, above = sides(ix, 15, x1_ref[at, :], x2_ref[at, :])
        pad_ref[f, 0:2, 8:40, :] = below.reshape(2, 32, 128)
        pad_ref[f, 10:12, 8:40, :] = above.reshape(2, 32, 128)
    below, above = sides(iy, 3, y1_ref[...], y2_ref[...])
    for h in range(2):
        for f in range(4):
            for i in range(8):
                n = h * 32 + f * 8 + i
                pad_ref[f, 2 + i, 6 + h:7 + h, :] = below[n:n + 1]
                pad_ref[f, 2 + i, 40 + h:41 + h, :] = above[n:n + 1]
    below, above = sides(iz, 3, z1_ref[...], z2_ref[...])
    for b in range(8):
        block = jnp.concatenate(
            [above[2 * b:2 * b + 2], jnp.zeros((124, 128), f32), below[2 * b:2 * b + 2]], axis=0
        )
        edge_ref[b // 2, (b % 2) * 4:(b % 2) * 4 + 4] = block.T.reshape(4, 32, 128)

    lane = lax.broadcasted_iota(i32, (8, 128), 1)

    def plane(i, carry):
        for c in range(4):
            j = 8 + 8 * c
            center, grads, laps = [], [], []
            for f in range(4):
                mid = pad_ref[f, i + 2, j:j + 8, :]
                edge = edge_ref[f, i, 8 * c:8 * c + 8, :]
                xs = [pad_ref[f, i + 2 + h, j:j + 8, :] for h in (-2, -1, 1, 2)]
                ys = [pad_ref[f, i + 2, j + h:j + 8 + h, :] for h in (-2, -1, 1, 2)]
                zs = [
                    pltpu.roll(jnp.where(lane >= 126, edge, mid), 2, 1),
                    pltpu.roll(jnp.where(lane >= 127, edge, mid), 1, 1),
                    pltpu.roll(jnp.where(lane < 1, edge, mid), 127, 1),
                    pltpu.roll(jnp.where(lane < 2, edge, mid), 126, 1),
                ]
                center.append(mid)
                grads.append([
                    ((m2 - p2) + 8.0 * (p1 - m1)) * (1.0 / 12.0) for m2, m1, p1, p2 in (xs, ys, zs)
                ])
                around = (xs[1] + xs[2]) + (ys[1] + ys[2]) + (zs[1] + zs[2])
                laps.append(around - 6.0 * mid)
            u, v, w, working = center
            curl_x = grads[2][1] - grads[1][2]
            curl_y = grads[0][2] - grads[2][0]
            curl_z = grads[1][0] - grads[0][1]
            rate = jnp.maximum(
                jnp.sqrt(curl_x * curl_x + curl_y * curl_y + curl_z * curl_z), floor_rate
            )
            positive = jnp.maximum(working, 0.0)
            chi = positive * (1.0 / viscosity)
            cubed = chi * chi * chi
            diffusion = viscosity + positive * cubed / (cubed + visc_coef**3)
            wall = wall_ref[i, 8 * c:8 * c + 8, :]
            arg = 8.0 * (diffusion / (rate * (karman * karman) * wall * wall))
            shield = 1.0 - jnp.tanh(arg * arg * arg)
            length = wall - shield * jnp.maximum(wall - des_coef, 0.0)
            convect = [u * g[0] + v * g[1] + w * g[2] for g in grads]
            gn = grads[3]
            grad_sq = gn[0] * gn[0] + gn[1] * gn[1] + gn[2] * gn[2]
            nu_rhs = (
                sigma_inv * ((viscosity + positive) * laps[3] + grad_coef * grad_sq)
                - convect[3]
                + prod_coef * rate * working
                - wall_coef * working * jnp.abs(working) / (length * length)
            )
            mask = fluid_ref[i, 8 * c:8 * c + 8, :].astype(f32) * time_step
            for f in range(3):
                vel_ref[f, i, 8 * c:8 * c + 8, :] = center[f] + mask * (diffusion * laps[f] - convect[f])
            nu_ref[i, 8 * c:8 * c + 8, :] = working + mask * nu_rhs
        return carry

    lax.fori_loop(0, 8, plane, 0, unroll=8)


def vmem():
    return pl.BlockSpec(memory_space=pltpu.VMEM)


def anywhere():
    return pl.BlockSpec(memory_space=pl.ANY)


def call(kernel, out_shape, in_specs, scratch, name, flops, moved, limit=VMEM_LIMIT):
    many = isinstance(out_shape, (list, tuple))
    return pl.pallas_call(
        kernel,
        out_shape=out_shape,
        in_specs=in_specs,
        out_specs=[vmem()] * len(out_shape) if many else vmem(),
        scratch_shapes=scratch,
        compiler_params=pltpu.CompilerParams(vmem_limit_bytes=limit),
        cost_estimate=pl.CostEstimate(flops=flops, bytes_accessed=moved, transcendentals=0),
        name=name,
    )


def exchange(block, axis, bit):
    count = lax.axis_size(axis)
    return lax.ppermute(block, axis, [(i, i ^ bit) for i in range(count)])


def swap_up(block, axis):
    return exchange(block, axis, 1)


def swap_down(block, axis):
    count = lax.axis_size(axis)
    return lax.ppermute(
        block, axis, [(i, (i + (1 if i % 2 else -1)) % count) for i in range(count)]
    )


def on_device(
    velocity, nu_tilde, fluid_cells, surface, pitch_angle, near_tiles, send_rows, ghost_cell,
    ghost_src, ghost_weight,
):
    shape = lambda *dims, dtype=f32: jax.ShapeDtypeStruct(dims, dtype)
    vel = velocity.reshape(3, ROWS, CZ)
    nu = nu_tilde.reshape(ROWS, CZ)
    cells = ghost_cell.reshape(16, 128)
    rows = send_rows.reshape(64, 128)
    outgoing = call(
        pack_kernel, shape(256, 128), [anywhere()] * 3,
        [pltpu.VMEM((512, 2 * ROWS), bf16),
         pltpu.VMEM((3, ROWS, CZ), f32), pltpu.VMEM((ROWS, CZ), f32), pltpu.VMEM((64, 128), i32),
         pltpu.VMEM((2, 512, 128), f32), pltpu.SemaphoreType.DMA((3,))],
        "pack_rows", 4_000_000_000, 1_000_000, 60 * 1024 * 1024,
    )(vel, nu, rows)
    points, outgoing = lax.optimization_barrier((surface.reshape(3, 1, 128), outgoing))
    incoming = lax.all_to_all(
        outgoing.reshape(256 * 128), ("gx", "gz"), split_axis=0, concat_axis=0, tiled=True
    ).reshape(256, 128)
    points = jnp.concatenate([points, exchange(points, "gy", 1)])
    far_points = exchange(points, "gy", 2)

    base, hot, low_hot = call(
        prepare_kernel,
        (shape(4, ROWS, CZ), shape(ROWS, 2048, dtype=bf16), shape(CZ, 2048, dtype=bf16)),
        [vmem()] * 3, [], "prepare", 200_000_000, 2_000_000,
    )(vel, nu, cells)
    points, base = lax.optimization_barrier((points, base))

    filled, x1, x2, y1, y2, z1, z2 = call(
        fill_kernel,
        (shape(4, ROWS, CZ), shape(256, 128), shape(256, 128), shape(64, 128), shape(64, 128),
         shape(16, 128), shape(16, 128)),
        [vmem()] * 6,
        [pltpu.VMEM((256, 256), bf16), pltpu.VMEM((1024, 2048), bf16),
         pltpu.VMEM((4 * ROWS, CZ), f32)],
        "fill_ghosts", 4_000_000_000, 2_000_000,
    )(incoming, ghost_src.reshape(8, 2048), ghost_weight.reshape(8, 2048), base, hot, low_hot)

    far_points, x1 = lax.optimization_barrier((far_points, x1))
    wall, wall_again = call(
        wall_kernel, (shape(32, TY, CZ), shape(32, TY, CZ)), [vmem()] * 4,
        [pltpu.VMEM((4, CZ, 128), f32), pltpu.VMEM((4, 8, 128), f32)], "wall", 30_000_000, 200_000,
    )(near_tiles.reshape(1, 8), pitch_angle.reshape(1, 1), points, far_points)

    x1, x2 = swap_up(x1, "gx"), swap_down(x2, "gx")
    y1, y2 = swap_up(y1, "gy"), swap_down(y2, "gy")
    z1 = swap_up(z1, "gz")
    z2, x1 = lax.optimization_barrier((z2, x1))
    z2 = swap_down(z2, "gz")

    wall = wall.reshape(CX, CY, CZ)
    new_velocity, new_nu = call(
        advance_kernel, (shape(3, CX, CY, CZ), shape(CX, CY, CZ)), [vmem()] * 9,
        [pltpu.VMEM((4, 12, 48, CZ), f32), pltpu.VMEM((4, CX, CY, CZ), f32)],
        "advance", 20_000_000, 3_000_000,
    )(filled, x1, x2, y1, y2, z1, z2, wall_again.reshape(CX, CY, CZ), fluid_cells)
    return new_velocity, new_nu, wall


def solution(mesh):
    in_specs = (
        P(None, "gx", "gy", "gz"),
        P("gx", "gy", "gz"),
        P("gx", "gy", "gz"),
        P("gx", "gz", None, "gy"),
        P(),
        P("gx", "gy", "gz", None),
        P("gx", "gy", "gz", None, None),
        P("gx", "gy", "gz", None),
        P("gx", "gy", "gz", None, None),
        P("gx", "gy", "gz", None, None),
    )
    out_specs = (P(None, "gx", "gy", "gz"), P("gx", "gy", "gz"), P("gx", "gy", "gz"))
    return jax.shard_map(
        on_device, mesh=mesh, in_specs=in_specs, out_specs=out_specs, check_vma=False
    )
```

```python
import jax
import jax.numpy as jnp
from jax import lax
from jax.experimental import pallas as pl
from jax.experimental.pallas import tpu as pltpu
from jax.sharding import PartitionSpec as P

f32 = jnp.float32
bf16 = jnp.bfloat16
i32 = jnp.int32

CX, CY, CZ = 8, 32, 128
ROWS = CX * CY
TY = 8

viscosity = 0.2
prod_coef = 0.1355
grad_coef = 0.622
sigma_inv = 1.5
karman = 0.41
visc_coef = 7.1
wall_coef = prod_coef / (karman * karman) + (1.0 + grad_coef) * sigma_inv
des_coef = 0.65
floor_rate = 0.3
dist_eps = 0.25
dist_cap = 8.0
time_step = 0.05

VMEM_LIMIT = 24 * 1024 * 1024


def in_two(values):
    high = values.astype(bf16)
    return high, (values - high.astype(f32)).astype(bf16)


def one_hot(index, count):
    level = lax.broadcasted_iota(i32, (count, 1), 0).astype(f32).astype(bf16)
    return jnp.where(level == index.astype(f32).astype(bf16), jnp.ones((), bf16), jnp.zeros((), bf16))


def pick_group(values, index):
    groups = values.shape[0]
    bit = 0
    while groups > 1:
        groups //= 2
        mask = ((index >> bit) & 1) == 1
        pairs = values.reshape((groups, 2) + values.shape[1:])
        values = jnp.where(mask[None], pairs[:, 1], pairs[:, 0])
        bit += 1
    return values[0]


def two_rows(ref, pair):
    return jnp.concatenate([ref[pl.ds(2 * pair, 1), :], ref[pl.ds(2 * pair + 1, 1), :]], axis=1)


def pack_kernel(
    vel_hbm, nu_hbm, rows_hbm, out_ref, table_ref, vel_ref, nu_ref, rows_ref, turn_ref, sems
):
    copies = [
        pltpu.make_async_copy(vel_hbm, vel_ref, sems.at[0]),
        pltpu.make_async_copy(nu_hbm, nu_ref, sems.at[1]),
        pltpu.make_async_copy(rows_hbm, rows_ref, sems.at[2]),
    ]
    for copy in copies:
        copy.start()
    copies[0].wait()
    for f in range(4):
        if f == 3:
            copies[1].wait()
        block = vel_ref[f] if f < 3 else nu_ref[...]
        for half in range(2):
            turn_ref[half, pl.ds(f, CZ, stride=4), :] = block[half * 128:half * 128 + 128].T
    for half in range(2):
        high, low = in_two(turn_ref[half])
        table_ref[:, half * 128:half * 128 + 128] = high
        table_ref[:, ROWS + half * 128:ROWS + half * 128 + 128] = low
    copies[2].wait()
    top = lax.broadcasted_iota(i32, (8, 128), 0) < 4

    def step(pair, carry):
        rows = two_rows(rows_ref, pair)
        hot = one_hot(rows >> 7, ROWS)
        found = jnp.dot(
            table_ref[...], jnp.concatenate([hot, hot], axis=0), preferred_element_type=f32
        )
        column = rows & 127
        both = pick_group(found.reshape(CZ // 2, 8, 256), column >> 1)
        swapped = jnp.concatenate([both[4:], both[:4]], axis=0)
        odd = (column & 1) == 1
        first = jnp.where(odd[:, :128], swapped[:, :128], both[:, :128])
        second = jnp.where(odd[:, 128:], both[:, 128:], swapped[:, 128:])
        out_ref[pl.ds(pl.multiple_of(pair * 8, 8), 8), :] = jnp.where(top, first, second)
        return carry

    lax.fori_loop(0, 32, step, 0, unroll=32)


def prepare_kernel(vel_ref, nu_ref, cell_ref, pitch_ref, base_ref, hot_ref, low_ref, trig_ref):
    angle = jnp.broadcast_to(pitch_ref[...], (1, 128))
    trig_ref[0:1, :] = jnp.cos(angle)
    trig_ref[1:2, :] = jnp.sin(angle)
    for pair in range(8):
        cell = two_rows(cell_ref, pair)
        hot_ref[:, pair * 256:(pair + 1) * 256] = one_hot(cell >> 7, ROWS)
        low_ref[:, pair * 256:(pair + 1) * 256] = one_hot(cell & 127, CZ)
    count = lax.dot_general(
        hot_ref[...], low_ref[...], (((1,), (1,)), ((), ())), preferred_element_type=f32
    )
    ghost = count > 0.5
    for f in range(4):
        block = vel_ref[f] if f < 3 else nu_ref[...]
        base_ref[f] = jnp.where(ghost, 0.0, block)


def turn_points(trig_ref, near_ref, far_ref, depth_ref):
    cosine, sine = trig_ref[0:1, :], trig_ref[1:2, :]
    depth = lax.broadcasted_iota(i32, (CZ, 128), 0).astype(f32) + (0.5 - 0.5 * CZ)
    turned = []
    for q, (ref, n) in enumerate(((near_ref, 0), (near_ref, 3), (far_ref, 0), (far_ref, 3))):
        x, y, z = ref[n], ref[n + 1], ref[n + 2]
        turned.append((cosine * x + sine * z, y))
        step_z = depth - (cosine * z - sine * x)
        depth_ref[q] = step_z * step_z
    return turned


def tile_at(tiles_ref, slot):
    return jnp.max(tiles_ref[:, slot:slot + 1].astype(f32)).astype(i32)


def tile_distance(tile, turned, depth_ref, span_ref):
    coord_x = (tile // 4).astype(f32) + (0.5 - 0.5 * CX)
    first = (tile % 4) * TY + lax.axis_index("gy") * CY
    coord_y = (lax.broadcasted_iota(i32, (8, 128), 0) + first).astype(f32) + (0.5 - 0.5 * 4 * CY)
    for q in range(4):
        step_x = coord_x - turned[q][0]
        step_y = coord_y - turned[q][1]
        span_ref[q] = step_x * step_x + step_y * step_y
    rows = []
    for r in range(8):
        least = None
        for q in range(4):
            here = span_ref[q, r:r + 1, :] + depth_ref[q]
            least = here if least is None else jnp.minimum(least, here)
        rows.append(jnp.min(least.T, axis=0, keepdims=True))
    return jnp.minimum(jnp.sqrt(jnp.concatenate(rows, axis=0) + dist_eps), dist_cap)


def wall_kernel(
    tiles_ref, trig_ref, near_ref, far_ref, wall_ref, again_ref, depth_ref, span_ref
):
    tiles = [tile_at(tiles_ref, slot) for slot in range(8)]
    turned = turn_points(trig_ref, near_ref, far_ref, depth_ref)
    wall_ref[...] = jnp.full(wall_ref.shape, dist_cap, f32)
    for slot in range(8):

        @pl.when(tiles[slot] >= 0)
        def _():
            wall_ref[tiles[slot]] = tile_distance(tiles[slot], turned, depth_ref, span_ref)

    again_ref[...] = wall_ref[...]


def fill_kernel(
    inc_ref, src_ref, weight_ref, base_ref, hot_ref, low_ref,
    filled_ref, x1_ref, x2_ref, y1_ref, y2_ref, z1_ref, z2_ref,
    table_ref, value_ref, flat_ref
):
    high, low = in_two(inc_ref[...])
    table_ref[:, :CZ] = high
    table_ref[:, CZ:] = low

    def step(block, carry):
        at = pl.ds(pl.multiple_of(block * 256, 256), 256)
        total = jnp.zeros((4, 256), f32)
        for t in range(8):
            source = src_ref[t:t + 1, at]
            hot = one_hot(source & 127, CZ)
            found = jnp.dot(
                table_ref[...], jnp.concatenate([hot, hot], axis=0), preferred_element_type=f32
            )
            peer = source >> 7
            both = pick_group(found.reshape(32, 8, 256), peer >> 1)
            value = jnp.where((peer & 1) == 1, both[4:], both[:4])
            total = total + weight_ref[t:t + 1, at] * value
        total = -total
        high = total.astype(bf16).astype(f32)
        rest = total - high
        low_hot = low_ref[:, at]
        for f in range(4):
            value_ref[pl.ds(f * CZ, CZ), at] = low_hot * high[f:f + 1].astype(bf16)
            value_ref[pl.ds((4 + f) * CZ, CZ), at] = low_hot * rest[f:f + 1].astype(bf16)
        return carry

    lax.fori_loop(0, 8, step, 0, unroll=8)
    added = lax.dot_general(
        hot_ref[...], value_ref[...], (((1,), (1,)), ((), ())), preferred_element_type=f32
    )
    added = added[:, :4 * CZ] + added[:, 4 * CZ:]
    even_x, even_y, even_z = [(lax.axis_index(axis) & 1) == 0 for axis in ("gx", "gy", "gz")]
    for f in range(4):
        block = base_ref[f] + added[:, f * CZ:(f + 1) * CZ]
        filled_ref[f] = block
        flat_ref[pl.ds(f * ROWS, ROWS), :] = block
        low, high = block[:64], block[ROWS - 64:]
        x1_ref[pl.ds(f * 64, 64), :] = jnp.where(even_x, high, low)
        x2_ref[pl.ds(f * 64, 64), :] = jnp.where(even_x, low, high)
    for h in range(2):
        low = flat_ref[pl.ds(h, 32, stride=32), :]
        high = flat_ref[pl.ds(30 + h, 32, stride=32), :]
        y1_ref[pl.ds(h * 32, 32), :] = jnp.where(even_y, high, low)
        y2_ref[pl.ds(h * 32, 32), :] = jnp.where(even_y, low, high)
    for b in range(8):
        turn = flat_ref[pl.ds(b * 128, 128), :].T
        z1_ref[pl.ds(b * 2, 2), :] = jnp.where(even_z, turn[126:128], turn[0:2])
        z2_ref[pl.ds(b * 2, 2), :] = jnp.where(even_z, turn[0:2], turn[126:128])


def advance_kernel(
    filled_ref, x1_ref, x2_ref, y1_ref, y2_ref, z1_ref, z2_ref, wall_ref, fluid_ref,
    vel_ref, nu_ref, pad_ref, edge_ref
):
    ix, iy, iz = lax.axis_index("gx"), lax.axis_index("gy"), lax.axis_index("gz")

    def sides(index, last, first, second):
        odd = (index & 1) == 1
        below = jnp.where(odd, first, second)
        above = jnp.where(odd, second, first)
        return jnp.where(index > 0, below, 0.0), jnp.where(index < last, above, 0.0)

    for f in range(4):
        pad_ref[f, 2:10, 8:40, :] = filled_ref[f].reshape(8, 32, 128)
        at = pl.ds(f * 64, 64)
        below, above = sides(ix, 15, x1_ref[at, :], x2_ref[at, :])
        pad_ref[f, 0:2, 8:40, :] = below.reshape(2, 32, 128)
        pad_ref[f, 10:12, 8:40, :] = above.reshape(2, 32, 128)
    below, above = sides(iy, 3, y1_ref[...], y2_ref[...])
    for h in range(2):
        for f in range(4):
            for i in range(8):
                n = h * 32 + f * 8 + i
                pad_ref[f, 2 + i, 6 + h:7 + h, :] = below[n:n + 1]
                pad_ref[f, 2 + i, 40 + h:41 + h, :] = above[n:n + 1]
    below, above = sides(iz, 3, z1_ref[...], z2_ref[...])
    for b in range(8):
        block = jnp.concatenate(
            [above[2 * b:2 * b + 2], jnp.zeros((124, 128), f32), below[2 * b:2 * b + 2]], axis=0
        )
        edge_ref[b // 2, (b % 2) * 4:(b % 2) * 4 + 4] = block.T.reshape(4, 32, 128)

    lane = lax.broadcasted_iota(i32, (8, 128), 1)

    def plane(i, carry):
        for c in range(4):
            j = 8 + 8 * c
            center, grads, laps = [], [], []
            for f in range(4):
                mid = pad_ref[f, i + 2, j:j + 8, :]
                edge = edge_ref[f, i, 8 * c:8 * c + 8, :]
                xs = [pad_ref[f, i + 2 + h, j:j + 8, :] for h in (-2, -1, 1, 2)]
                ys = [pad_ref[f, i + 2, j + h:j + 8 + h, :] for h in (-2, -1, 1, 2)]
                zs = [
                    pltpu.roll(jnp.where(lane >= 126, edge, mid), 2, 1),
                    pltpu.roll(jnp.where(lane >= 127, edge, mid), 1, 1),
                    pltpu.roll(jnp.where(lane < 1, edge, mid), 127, 1),
                    pltpu.roll(jnp.where(lane < 2, edge, mid), 126, 1),
                ]
                center.append(mid)
                grads.append([
                    ((m2 - p2) + 8.0 * (p1 - m1)) * (1.0 / 12.0) for m2, m1, p1, p2 in (xs, ys, zs)
                ])
                around = (xs[1] + xs[2]) + (ys[1] + ys[2]) + (zs[1] + zs[2])
                laps.append(around - 6.0 * mid)
            u, v, w, working = center
            curl_x = grads[2][1] - grads[1][2]
            curl_y = grads[0][2] - grads[2][0]
            curl_z = grads[1][0] - grads[0][1]
            rate = jnp.maximum(
                jnp.sqrt(curl_x * curl_x + curl_y * curl_y + curl_z * curl_z), floor_rate
            )
            positive = jnp.maximum(working, 0.0)
            chi = positive * (1.0 / viscosity)
            cubed = chi * chi * chi
            diffusion = viscosity + positive * cubed / (cubed + visc_coef**3)
            wall = wall_ref[i, 8 * c:8 * c + 8, :]
            arg = 8.0 * (diffusion / (rate * (karman * karman) * wall * wall))
            shield = 1.0 - jnp.tanh(arg * arg * arg)
            length = wall - shield * jnp.maximum(wall - des_coef, 0.0)
            convect = [u * g[0] + v * g[1] + w * g[2] for g in grads]
            gn = grads[3]
            grad_sq = gn[0] * gn[0] + gn[1] * gn[1] + gn[2] * gn[2]
            nu_rhs = (
                sigma_inv * ((viscosity + positive) * laps[3] + grad_coef * grad_sq)
                - convect[3]
                + prod_coef * rate * working
                - wall_coef * working * jnp.abs(working) / (length * length)
            )
            mask = fluid_ref[i, 8 * c:8 * c + 8, :].astype(f32) * time_step
            for f in range(3):
                vel_ref[f, i, 8 * c:8 * c + 8, :] = center[f] + mask * (diffusion * laps[f] - convect[f])
            nu_ref[i, 8 * c:8 * c + 8, :] = working + mask * nu_rhs
        return carry

    lax.fori_loop(0, 8, plane, 0, unroll=8)


def vmem():
    return pl.BlockSpec(memory_space=pltpu.VMEM)


def anywhere():
    return pl.BlockSpec(memory_space=pl.ANY)


def call(kernel, out_shape, in_specs, scratch, name, flops, moved, limit=VMEM_LIMIT):
    many = isinstance(out_shape, (list, tuple))
    return pl.pallas_call(
        kernel,
        out_shape=out_shape,
        in_specs=in_specs,
        out_specs=[vmem()] * len(out_shape) if many else vmem(),
        scratch_shapes=scratch,
        compiler_params=pltpu.CompilerParams(vmem_limit_bytes=limit),
        cost_estimate=pl.CostEstimate(flops=flops, bytes_accessed=moved, transcendentals=0),
        name=name,
    )


def exchange(block, axis, bit):
    count = lax.axis_size(axis)
    return lax.ppermute(block, axis, [(i, i ^ bit) for i in range(count)])


def swap_up(block, axis):
    return exchange(block, axis, 1)


def swap_down(block, axis):
    count = lax.axis_size(axis)
    return lax.ppermute(
        block, axis, [(i, (i + (1 if i % 2 else -1)) % count) for i in range(count)]
    )


def on_device(
    velocity, nu_tilde, fluid_cells, surface, pitch_angle, near_tiles, send_rows, ghost_cell,
    ghost_src, ghost_weight,
):
    shape = lambda *dims, dtype=f32: jax.ShapeDtypeStruct(dims, dtype)
    vel = velocity.reshape(3, ROWS, CZ)
    nu = nu_tilde.reshape(ROWS, CZ)
    cells = ghost_cell.reshape(16, 128)
    rows = send_rows.reshape(64, 128)
    outgoing = call(
        pack_kernel, shape(256, 128), [anywhere()] * 3,
        [pltpu.VMEM((512, 2 * ROWS), bf16),
         pltpu.VMEM((3, ROWS, CZ), f32), pltpu.VMEM((ROWS, CZ), f32), pltpu.VMEM((64, 128), i32),
         pltpu.VMEM((2, 512, 128), f32), pltpu.SemaphoreType.DMA((3,))],
        "pack_rows", 4_000_000_000, 1_000_000, 60 * 1024 * 1024,
    )(vel, nu, rows)
    points, outgoing = lax.optimization_barrier((surface.reshape(3, 1, 128), outgoing))
    incoming = lax.all_to_all(
        outgoing.reshape(256 * 128), ("gx", "gz"), split_axis=0, concat_axis=0, tiled=True
    ).reshape(256, 128)
    points = jnp.concatenate([points, exchange(points, "gy", 1)])
    far_points = exchange(points, "gy", 2)

    base, hot, low_hot, trig = call(
        prepare_kernel,
        (shape(4, ROWS, CZ), shape(ROWS, 2048, dtype=bf16), shape(CZ, 2048, dtype=bf16),
         shape(2, 128)),
        [vmem()] * 4, [], "prepare", 200_000_000, 2_000_000,
    )(vel, nu, cells, pitch_angle.reshape(1, 1))
    points, base = lax.optimization_barrier((points, base))

    filled, x1, x2, y1, y2, z1, z2 = call(
        fill_kernel,
        (shape(4, ROWS, CZ), shape(256, 128), shape(256, 128), shape(64, 128), shape(64, 128),
         shape(16, 128), shape(16, 128)),
        [vmem()] * 6,
        [pltpu.VMEM((256, 256), bf16), pltpu.VMEM((1024, 2048), bf16),
         pltpu.VMEM((4 * ROWS, CZ), f32)],
        "fill_ghosts", 4_000_000_000, 2_000_000,
    )(incoming, ghost_src.reshape(8, 2048), ghost_weight.reshape(8, 2048), base, hot, low_hot)

    far_points, x1 = lax.optimization_barrier((far_points, x1))
    wall, wall_again = call(
        wall_kernel, (shape(32, TY, CZ), shape(32, TY, CZ)), [vmem()] * 4,
        [pltpu.VMEM((4, CZ, 128), f32), pltpu.VMEM((4, 8, 128), f32)], "wall", 30_000_000, 200_000,
    )(near_tiles.reshape(1, 8), trig, points, far_points)

    x1, x2 = swap_up(x1, "gx"), swap_down(x2, "gx")
    y1, y2 = swap_up(y1, "gy"), swap_down(y2, "gy")
    z1 = swap_up(z1, "gz")
    z2, x1 = lax.optimization_barrier((z2, x1))
    z2 = swap_down(z2, "gz")

    wall = wall.reshape(CX, CY, CZ)
    new_velocity, new_nu = call(
        advance_kernel, (shape(3, CX, CY, CZ), shape(CX, CY, CZ)), [vmem()] * 9,
        [pltpu.VMEM((4, 12, 48, CZ), f32), pltpu.VMEM((4, CX, CY, CZ), f32)],
        "advance", 20_000_000, 3_000_000,
    )(filled, x1, x2, y1, y2, z1, z2, wall_again.reshape(CX, CY, CZ), fluid_cells)
    return new_velocity, new_nu, wall


def solution(mesh):
    in_specs = (
        P(None, "gx", "gy", "gz"),
        P("gx", "gy", "gz"),
        P("gx", "gy", "gz"),
        P("gx", "gz", None, "gy"),
        P(),
        P("gx", "gy", "gz", None),
        P("gx", "gy", "gz", None, None),
        P("gx", "gy", "gz", None),
        P("gx", "gy", "gz", None, None),
        P("gx", "gy", "gz", None, None),
    )
    out_specs = (P(None, "gx", "gy", "gz"), P("gx", "gy", "gz"), P("gx", "gy", "gz"))
    return jax.shard_map(
        on_device, mesh=mesh, in_specs=in_specs, out_specs=out_specs, check_vma=False
    )
```

```python
import jax
import jax.numpy as jnp
from jax import lax
from jax.experimental import pallas as pl
from jax.experimental.pallas import tpu as pltpu
from jax.sharding import PartitionSpec as P

f32 = jnp.float32
bf16 = jnp.bfloat16
i32 = jnp.int32

CX, CY, CZ = 8, 32, 128
ROWS = CX * CY
TY = 8

viscosity = 0.2
prod_coef = 0.1355
grad_coef = 0.622
sigma_inv = 1.5
karman = 0.41
visc_coef = 7.1
wall_coef = prod_coef / (karman * karman) + (1.0 + grad_coef) * sigma_inv
des_coef = 0.65
floor_rate = 0.3
dist_eps = 0.25
dist_cap = 8.0
time_step = 0.05

VMEM_LIMIT = 24 * 1024 * 1024


def in_two(values):
    high = values.astype(bf16)
    return high, (values - high.astype(f32)).astype(bf16)


def one_hot(index, count):
    level = lax.broadcasted_iota(i32, (count, 1), 0).astype(f32).astype(bf16)
    return jnp.where(level == index.astype(f32).astype(bf16), jnp.ones((), bf16), jnp.zeros((), bf16))


def pick_group(values, index):
    groups = values.shape[0]
    bit = 0
    while groups > 1:
        groups //= 2
        mask = ((index >> bit) & 1) == 1
        pairs = values.reshape((groups, 2) + values.shape[1:])
        values = jnp.where(mask[None], pairs[:, 1], pairs[:, 0])
        bit += 1
    return values[0]


def two_rows(ref, pair):
    return jnp.concatenate([ref[pl.ds(2 * pair, 1), :], ref[pl.ds(2 * pair + 1, 1), :]], axis=1)


def pack_kernel(
    vel_hbm, nu_hbm, rows_hbm, out_ref, table_ref, vel_ref, nu_ref, rows_ref, turn_ref, sems
):
    copies = [
        pltpu.make_async_copy(vel_hbm.at[0], vel_ref.at[0], sems.at[0]),
        pltpu.make_async_copy(vel_hbm.at[1], vel_ref.at[1], sems.at[1]),
        pltpu.make_async_copy(vel_hbm.at[2], vel_ref.at[2], sems.at[2]),
        pltpu.make_async_copy(nu_hbm, nu_ref, sems.at[3]),
        pltpu.make_async_copy(rows_hbm, rows_ref, sems.at[4]),
    ]
    for copy in copies:
        copy.start()
    for f in range(4):
        copies[f].wait()
        block = vel_ref[f] if f < 3 else nu_ref[...]
        for half in range(2):
            turn_ref[half, pl.ds(f, CZ, stride=4), :] = block[half * 128:half * 128 + 128].T
    for half in range(2):
        high, low = in_two(turn_ref[half])
        table_ref[:, half * 128:half * 128 + 128] = high
        table_ref[:, ROWS + half * 128:ROWS + half * 128 + 128] = low
    copies[4].wait()
    top = lax.broadcasted_iota(i32, (8, 128), 0) < 4

    def step(pair, carry):
        rows = two_rows(rows_ref, pair)
        hot = one_hot(rows >> 7, ROWS)
        found = jnp.dot(
            table_ref[...], jnp.concatenate([hot, hot], axis=0), preferred_element_type=f32
        )
        column = rows & 127
        both = pick_group(found.reshape(CZ // 2, 8, 256), column >> 1)
        swapped = jnp.concatenate([both[4:], both[:4]], axis=0)
        odd = (column & 1) == 1
        first = jnp.where(odd[:, :128], swapped[:, :128], both[:, :128])
        second = jnp.where(odd[:, 128:], both[:, 128:], swapped[:, 128:])
        out_ref[pl.ds(pl.multiple_of(pair * 8, 8), 8), :] = jnp.where(top, first, second)
        return carry

    lax.fori_loop(0, 32, step, 0, unroll=32)


def prepare_kernel(vel_ref, nu_ref, cell_ref, base_ref, hot_ref, low_ref):
    for pair in range(8):
        cell = two_rows(cell_ref, pair)
        hot_ref[:, pair * 256:(pair + 1) * 256] = one_hot(cell >> 7, ROWS)
        low_ref[:, pair * 256:(pair + 1) * 256] = one_hot(cell & 127, CZ)
    count = lax.dot_general(
        hot_ref[...], low_ref[...], (((1,), (1,)), ((), ())), preferred_element_type=f32
    )
    ghost = count > 0.5
    for f in range(4):
        block = vel_ref[f] if f < 3 else nu_ref[...]
        base_ref[f] = jnp.where(ghost, 0.0, block)


def turn_points(pitch_ref, near_ref, far_ref, depth_ref):
    angle = jnp.broadcast_to(pitch_ref[...], (1, 128))
    cosine = jnp.cos(angle)
    sine = jnp.sin(angle)
    depth = lax.broadcasted_iota(i32, (CZ, 128), 0).astype(f32) + (0.5 - 0.5 * CZ)
    turned = []
    for q, (ref, n) in enumerate(((near_ref, 0), (near_ref, 3), (far_ref, 0), (far_ref, 3))):
        x, y, z = ref[n], ref[n + 1], ref[n + 2]
        turned.append((cosine * x + sine * z, y))
        step_z = depth - (cosine * z - sine * x)
        depth_ref[q] = step_z * step_z
    return turned


def tile_at(tiles_ref, slot):
    return jnp.max(tiles_ref[:, slot:slot + 1].astype(f32)).astype(i32)


def tile_distance(tile, turned, depth_ref, span_ref):
    coord_x = (tile // 4).astype(f32) + (0.5 - 0.5 * CX)
    first = (tile % 4) * TY + lax.axis_index("gy") * CY
    coord_y = (lax.broadcasted_iota(i32, (8, 128), 0) + first).astype(f32) + (0.5 - 0.5 * 4 * CY)
    for q in range(4):
        step_x = coord_x - turned[q][0]
        step_y = coord_y - turned[q][1]
        span_ref[q] = step_x * step_x + step_y * step_y
    rows = []
    for r in range(8):
        least = None
        for q in range(4):
            here = span_ref[q, r:r + 1, :] + depth_ref[q]
            least = here if least is None else jnp.minimum(least, here)
        rows.append(jnp.min(least.T, axis=0, keepdims=True))
    return jnp.minimum(jnp.sqrt(jnp.concatenate(rows, axis=0) + dist_eps), dist_cap)


def wall_kernel(
    tiles_ref, pitch_ref, near_ref, far_ref, wall_ref, again_ref, depth_ref, span_ref
):
    tiles = [tile_at(tiles_ref, slot) for slot in range(8)]
    turned = turn_points(pitch_ref, near_ref, far_ref, depth_ref)
    wall_ref[...] = jnp.full(wall_ref.shape, dist_cap, f32)
    for slot in range(8):

        @pl.when(tiles[slot] >= 0)
        def _():
            wall_ref[tiles[slot]] = tile_distance(tiles[slot], turned, depth_ref, span_ref)

    again_ref[...] = wall_ref[...]


def fill_kernel(
    inc_ref, src_ref, weight_ref, base_ref, hot_ref, low_ref,
    filled_ref, x1_ref, x2_ref, y1_ref, y2_ref, z1_ref, z2_ref,
    table_ref, value_ref, flat_ref
):
    high, low = in_two(inc_ref[...])
    table_ref[:, :CZ] = high
    table_ref[:, CZ:] = low

    def step(block, carry):
        at = pl.ds(pl.multiple_of(block * 256, 256), 256)
        total = jnp.zeros((4, 256), f32)
        for t in range(8):
            source = src_ref[t:t + 1, at]
            hot = one_hot(source & 127, CZ)
            found = jnp.dot(
                table_ref[...], jnp.concatenate([hot, hot], axis=0), preferred_element_type=f32
            )
            peer = source >> 7
            both = pick_group(found.reshape(32, 8, 256), peer >> 1)
            value = jnp.where((peer & 1) == 1, both[4:], both[:4])
            total = total + weight_ref[t:t + 1, at] * value
        total = -total
        high = total.astype(bf16).astype(f32)
        rest = total - high
        low_hot = low_ref[:, at]
        for f in range(4):
            value_ref[pl.ds(f * CZ, CZ), at] = low_hot * high[f:f + 1].astype(bf16)
            value_ref[pl.ds((4 + f) * CZ, CZ), at] = low_hot * rest[f:f + 1].astype(bf16)
        return carry

    lax.fori_loop(0, 8, step, 0, unroll=8)
    added = lax.dot_general(
        hot_ref[...], value_ref[...], (((1,), (1,)), ((), ())), preferred_element_type=f32
    )
    added = added[:, :4 * CZ] + added[:, 4 * CZ:]
    even_x, even_y, even_z = [(lax.axis_index(axis) & 1) == 0 for axis in ("gx", "gy", "gz")]
    for f in range(4):
        block = base_ref[f] + added[:, f * CZ:(f + 1) * CZ]
        filled_ref[f] = block
        flat_ref[pl.ds(f * ROWS, ROWS), :] = block
        low, high = block[:64], block[ROWS - 64:]
        x1_ref[pl.ds(f * 64, 64), :] = jnp.where(even_x, high, low)
        x2_ref[pl.ds(f * 64, 64), :] = jnp.where(even_x, low, high)
    for h in range(2):
        low = flat_ref[pl.ds(h, 32, stride=32), :]
        high = flat_ref[pl.ds(30 + h, 32, stride=32), :]
        y1_ref[pl.ds(h * 32, 32), :] = jnp.where(even_y, high, low)
        y2_ref[pl.ds(h * 32, 32), :] = jnp.where(even_y, low, high)
    for b in range(8):
        turn = flat_ref[pl.ds(b * 128, 128), :].T
        z1_ref[pl.ds(b * 2, 2), :] = jnp.where(even_z, turn[126:128], turn[0:2])
        z2_ref[pl.ds(b * 2, 2), :] = jnp.where(even_z, turn[0:2], turn[126:128])


def advance_kernel(
    filled_ref, x1_ref, x2_ref, y1_ref, y2_ref, z1_ref, z2_ref, wall_ref, fluid_ref,
    vel_ref, nu_ref, pad_ref, edge_ref
):
    ix, iy, iz = lax.axis_index("gx"), lax.axis_index("gy"), lax.axis_index("gz")

    def sides(index, last, first, second):
        odd = (index & 1) == 1
        below = jnp.where(odd, first, second)
        above = jnp.where(odd, second, first)
        return jnp.where(index > 0, below, 0.0), jnp.where(index < last, above, 0.0)

    for f in range(4):
        pad_ref[f, 2:10, 8:40, :] = filled_ref[f].reshape(8, 32, 128)
        at = pl.ds(f * 64, 64)
        below, above = sides(ix, 15, x1_ref[at, :], x2_ref[at, :])
        pad_ref[f, 0:2, 8:40, :] = below.reshape(2, 32, 128)
        pad_ref[f, 10:12, 8:40, :] = above.reshape(2, 32, 128)
    below, above = sides(iy, 3, y1_ref[...], y2_ref[...])
    for h in range(2):
        for f in range(4):
            for i in range(8):
                n = h * 32 + f * 8 + i
                pad_ref[f, 2 + i, 6 + h:7 + h, :] = below[n:n + 1]
                pad_ref[f, 2 + i, 40 + h:41 + h, :] = above[n:n + 1]
    below, above = sides(iz, 3, z1_ref[...], z2_ref[...])
    for b in range(8):
        block = jnp.concatenate(
            [above[2 * b:2 * b + 2], jnp.zeros((124, 128), f32), below[2 * b:2 * b + 2]], axis=0
        )
        edge_ref[b // 2, (b % 2) * 4:(b % 2) * 4 + 4] = block.T.reshape(4, 32, 128)

    lane = lax.broadcasted_iota(i32, (8, 128), 1)

    def plane(i, carry):
        for c in range(4):
            j = 8 + 8 * c
            center, grads, laps = [], [], []
            for f in range(4):
                mid = pad_ref[f, i + 2, j:j + 8, :]
                edge = edge_ref[f, i, 8 * c:8 * c + 8, :]
                xs = [pad_ref[f, i + 2 + h, j:j + 8, :] for h in (-2, -1, 1, 2)]
                ys = [pad_ref[f, i + 2, j + h:j + 8 + h, :] for h in (-2, -1, 1, 2)]
                zs = [
                    pltpu.roll(jnp.where(lane >= 126, edge, mid), 2, 1),
                    pltpu.roll(jnp.where(lane >= 127, edge, mid), 1, 1),
                    pltpu.roll(jnp.where(lane < 1, edge, mid), 127, 1),
                    pltpu.roll(jnp.where(lane < 2, edge, mid), 126, 1),
                ]
                center.append(mid)
                grads.append([
                    ((m2 - p2) + 8.0 * (p1 - m1)) * (1.0 / 12.0) for m2, m1, p1, p2 in (xs, ys, zs)
                ])
                around = (xs[1] + xs[2]) + (ys[1] + ys[2]) + (zs[1] + zs[2])
                laps.append(around - 6.0 * mid)
            u, v, w, working = center
            curl_x = grads[2][1] - grads[1][2]
            curl_y = grads[0][2] - grads[2][0]
            curl_z = grads[1][0] - grads[0][1]
            rate = jnp.maximum(
                jnp.sqrt(curl_x * curl_x + curl_y * curl_y + curl_z * curl_z), floor_rate
            )
            positive = jnp.maximum(working, 0.0)
            chi = positive * (1.0 / viscosity)
            cubed = chi * chi * chi
            diffusion = viscosity + positive * cubed / (cubed + visc_coef**3)
            wall = wall_ref[i, 8 * c:8 * c + 8, :]
            arg = 8.0 * (diffusion / (rate * (karman * karman) * wall * wall))
            shield = 1.0 - jnp.tanh(arg * arg * arg)
            length = wall - shield * jnp.maximum(wall - des_coef, 0.0)
            convect = [u * g[0] + v * g[1] + w * g[2] for g in grads]
            gn = grads[3]
            grad_sq = gn[0] * gn[0] + gn[1] * gn[1] + gn[2] * gn[2]
            nu_rhs = (
                sigma_inv * ((viscosity + positive) * laps[3] + grad_coef * grad_sq)
                - convect[3]
                + prod_coef * rate * working
                - wall_coef * working * jnp.abs(working) / (length * length)
            )
            mask = fluid_ref[i, 8 * c:8 * c + 8, :].astype(f32) * time_step
            for f in range(3):
                vel_ref[f, i, 8 * c:8 * c + 8, :] = center[f] + mask * (diffusion * laps[f] - convect[f])
            nu_ref[i, 8 * c:8 * c + 8, :] = working + mask * nu_rhs
        return carry

    lax.fori_loop(0, 8, plane, 0, unroll=8)


def vmem():
    return pl.BlockSpec(memory_space=pltpu.VMEM)


def anywhere():
    return pl.BlockSpec(memory_space=pl.ANY)


def call(kernel, out_shape, in_specs, scratch, name, flops, moved, limit=VMEM_LIMIT):
    many = isinstance(out_shape, (list, tuple))
    return pl.pallas_call(
        kernel,
        out_shape=out_shape,
        in_specs=in_specs,
        out_specs=[vmem()] * len(out_shape) if many else vmem(),
        scratch_shapes=scratch,
        compiler_params=pltpu.CompilerParams(vmem_limit_bytes=limit),
        cost_estimate=pl.CostEstimate(flops=flops, bytes_accessed=moved, transcendentals=0),
        name=name,
    )


def exchange(block, axis, bit):
    count = lax.axis_size(axis)
    return lax.ppermute(block, axis, [(i, i ^ bit) for i in range(count)])


def swap_up(block, axis):
    return exchange(block, axis, 1)


def swap_down(block, axis):
    count = lax.axis_size(axis)
    return lax.ppermute(
        block, axis, [(i, (i + (1 if i % 2 else -1)) % count) for i in range(count)]
    )


def on_device(
    velocity, nu_tilde, fluid_cells, surface, pitch_angle, near_tiles, send_rows, ghost_cell,
    ghost_src, ghost_weight,
):
    shape = lambda *dims, dtype=f32: jax.ShapeDtypeStruct(dims, dtype)
    vel = velocity.reshape(3, ROWS, CZ)
    nu = nu_tilde.reshape(ROWS, CZ)
    cells = ghost_cell.reshape(16, 128)
    rows = send_rows.reshape(64, 128)
    outgoing = call(
        pack_kernel, shape(256, 128), [anywhere()] * 3,
        [pltpu.VMEM((512, 2 * ROWS), bf16),
         pltpu.VMEM((3, ROWS, CZ), f32), pltpu.VMEM((ROWS, CZ), f32), pltpu.VMEM((64, 128), i32),
         pltpu.VMEM((2, 512, 128), f32), pltpu.SemaphoreType.DMA((5,))],
        "pack_rows", 4_000_000_000, 1_000_000, 60 * 1024 * 1024,
    )(vel, nu, rows)
    points, outgoing = lax.optimization_barrier((surface.reshape(3, 1, 128), outgoing))
    incoming = lax.all_to_all(
        outgoing.reshape(256 * 128), ("gx", "gz"), split_axis=0, concat_axis=0, tiled=True
    ).reshape(256, 128)
    points = jnp.concatenate([points, exchange(points, "gy", 1)])
    far_points = exchange(points, "gy", 2)

    base, hot, low_hot = call(
        prepare_kernel,
        (shape(4, ROWS, CZ), shape(ROWS, 2048, dtype=bf16), shape(CZ, 2048, dtype=bf16)),
        [vmem()] * 3, [], "prepare", 200_000_000, 2_000_000,
    )(vel, nu, cells)
    points, base = lax.optimization_barrier((points, base))

    filled, x1, x2, y1, y2, z1, z2 = call(
        fill_kernel,
        (shape(4, ROWS, CZ), shape(256, 128), shape(256, 128), shape(64, 128), shape(64, 128),
         shape(16, 128), shape(16, 128)),
        [vmem()] * 6,
        [pltpu.VMEM((256, 256), bf16), pltpu.VMEM((1024, 2048), bf16),
         pltpu.VMEM((4 * ROWS, CZ), f32)],
        "fill_ghosts", 4_000_000_000, 2_000_000,
    )(incoming, ghost_src.reshape(8, 2048), ghost_weight.reshape(8, 2048), base, hot, low_hot)

    far_points, x1 = lax.optimization_barrier((far_points, x1))
    wall, wall_again = call(
        wall_kernel, (shape(32, TY, CZ), shape(32, TY, CZ)), [vmem()] * 4,
        [pltpu.VMEM((4, CZ, 128), f32), pltpu.VMEM((4, 8, 128), f32)], "wall", 30_000_000, 200_000,
    )(near_tiles.reshape(1, 8), pitch_angle.reshape(1, 1), points, far_points)

    x1, x2 = swap_up(x1, "gx"), swap_down(x2, "gx")
    y1, y2 = swap_up(y1, "gy"), swap_down(y2, "gy")
    z1 = swap_up(z1, "gz")
    z2, x1 = lax.optimization_barrier((z2, x1))
    z2 = swap_down(z2, "gz")

    wall = wall.reshape(CX, CY, CZ)
    new_velocity, new_nu = call(
        advance_kernel, (shape(3, CX, CY, CZ), shape(CX, CY, CZ)), [vmem()] * 9,
        [pltpu.VMEM((4, 12, 48, CZ), f32), pltpu.VMEM((4, CX, CY, CZ), f32)],
        "advance", 20_000_000, 3_000_000,
    )(filled, x1, x2, y1, y2, z1, z2, wall_again.reshape(CX, CY, CZ), fluid_cells)
    return new_velocity, new_nu, wall


def solution(mesh):
    in_specs = (
        P(None, "gx", "gy", "gz"),
        P("gx", "gy", "gz"),
        P("gx", "gy", "gz"),
        P("gx", "gz", None, "gy"),
        P(),
        P("gx", "gy", "gz", None),
        P("gx", "gy", "gz", None, None),
        P("gx", "gy", "gz", None),
        P("gx", "gy", "gz", None, None),
        P("gx", "gy", "gz", None, None),
    )
    out_specs = (P(None, "gx", "gy", "gz"), P("gx", "gy", "gz"), P("gx", "gy", "gz"))
    return jax.shard_map(
        on_device, mesh=mesh, in_specs=in_specs, out_specs=out_specs, check_vma=False
    )
```
